128 devices in a mesh: grp: 8 (over z, core), row: 16 (over x, y).
Axes of the slice: x: 4, y: 4, z: 4, core: 2. Of those that a mesh axis runs over, the one named last changes fastest.
Arguments:
- embeddings: bfloat16 [32768, 4096], P(('grp', 'row')), may hold values from -6 to 6
- member_order: int32 [32768], P(('grp', 'row')), may hold values from 0 to 8191, as said below
- member_count: int32 [4], replicated, may hold values from 2048 to 8192, as said below
Outputs:
- nearest: float32 [32768], P(('grp', 'row'))
The draws below stay inside these ranges and needn't reach their ends.
Inputs may be any that keep to these rules, and one draw needn't show every extreme that they name: `member_order`: each cluster's 8192 slots carry every rank of 0 to 8191 once. `member_count`: one cluster is full.
All inputs are finite; a program needn't handle non-finite values.
Results may differ from the reference program's by a relative error of at most 0.0003.
Values may be sent and summed in bfloat16 or wider, within the bound.
A program may use at most 128 MiB of HBM per device.

```python
import jax
import jax.numpy as jnp
from jax import lax

D = 4096
R = 256
CLUSTERS = 4
CLUSTER_ROWS = 8192
TOTAL = 32768


def draw_member_order(key, part):
    key = jax.random.fold_in(key, 11)
    keys = jax.random.split(key, CLUSTERS)
    perms = jax.vmap(lambda single: jax.random.permutation(single, CLUSTER_ROWS))(keys)
    return perms.reshape(-1).astype(jnp.int32)


def draw_member_count(key, part):
    key = jax.random.fold_in(key, 23)
    first, second = jax.random.split(key)
    counts = jax.random.randint(first, (CLUSTERS,), CLUSTER_ROWS // 4, CLUSTER_ROWS + 1)
    chosen = jax.random.randint(second, (), 0, CLUSTERS)
    counts = jnp.where(jnp.arange(CLUSTERS) == chosen, CLUSTER_ROWS, counts)
    return counts.astype(jnp.int32)


def levels(stream_key, dims, pieces, low, top_value):
    def one(position, blocks):
        heights = jax.random.uniform(jax.random.fold_in(jax.random.fold_in(stream_key, 6), position), (blocks,), jnp.float32, low / len(pieces), top_value / len(pieces))
        return jnp.repeat(jnp.exp(heights), dims[position] // blocks).reshape((-1,) + (1,) * (len(dims) - position - 1))

    gain = one(*pieces[0])
    for cut in pieces[1:]:
        gain = gain * one(*cut)
    return gain


def noise(own_key, dims, width, reach, shards=(), kind=jnp.bfloat16):
    values = jax.random.normal(own_key, dims, jnp.float32) * width
    if len(shards) > 0:
        values = levels(own_key, dims, shards, -0.22, 0.18) * values
    return jnp.clip(values, min=-reach, max=reach).astype(kind)


def setup_inputs(seed: int = 0) -> dict:
    key_of = jax.random.split(jax.random.key(seed), 4)
    return {
        "embeddings": noise(key_of[0], (TOTAL, D), 1.0, 6.0, ((0, 128),)),
        "member_order": draw_member_order(jax.random.fold_in(key_of[3], 71), 0),
        "member_count": draw_member_count(jax.random.fold_in(key_of[3], 71), 0),
    }


def reference(embeddings, member_order, member_count):
    values = embeddings.astype(jnp.float32)
    squares = lax.optimization_barrier(jnp.sum(values * values, axis=1, keepdims=True))
    unit = (values * lax.rsqrt(squares + 1e-06)).astype(jnp.bfloat16)
    unit_c = unit.reshape(CLUSTERS, CLUSTER_ROWS, D)
    order_c = member_order.reshape(CLUSTERS, CLUSTER_ROWS)
    slots = jnp.arange(CLUSTER_ROWS, dtype=jnp.int32)

    def one_cluster(packed):
        unit_k, order_k, count_k = packed
        live = slots < count_k
        blocks = unit_k.reshape(CLUSTER_ROWS // R, R, D)
        orders = order_k.reshape(CLUSTER_ROWS // R, R)

        def one_block(item):
            queries, query_order = item
            scores = lax.dot_general(queries, unit_k, (((1,), (1,)), ((), ())), preferred_element_type=jnp.float32)
            allowed = live[None, :] & (order_k[None, :] < query_order[:, None])
            return jnp.maximum(lax.optimization_barrier(jnp.max(jnp.where(allowed, scores, -1.0), axis=1)), -1.0)
        best = lax.map(one_block, (blocks, orders)).reshape(CLUSTER_ROWS)
        return jnp.where(live, best, jnp.float32(-1.0))
    result = lax.map(one_cluster, (unit_c, order_c, member_count.astype(jnp.int32)))
    return result.reshape(TOTAL)
```

```python
import jax
import jax.numpy as jnp
from jax import lax
from jax.experimental import pallas as pl
from jax.experimental.pallas import tpu as pltpu
from jax.sharding import PartitionSpec as P

MESH = pl.DeviceIdType.MESH
SIDE = 4
ROWS = 256
HALF = ROWS // 2
CHUNK = 64
CHUNKS = ROWS // CHUNK
EMPTY = 1 << 20
NEAR, FAR, OTHER = 4, 5, 6
SLOTS = 10


def kernel(
    rows_hbm, rank_ref, out_ref, blocks, rank_lane, rank_row, best_row, best_lane, mail, load_sem, send_sem, recv_sem,
    rank_send, rank_recv, mail_send, mail_recv,
):
    group, place = lax.axis_index("grp"), lax.axis_index("row")
    core = lax.rem(group, 2)
    x, y = place // SIDE, lax.rem(place, SIDE)

    def device(main, side, flip=False):
        dx = main * (1 - core) + side * core
        dy = main * core + side * (1 - core)
        there = lax.rem(x + dx + SIDE, SIDE) * SIDE + lax.rem(y + dy + SIDE, SIDE)
        return (group + 1 - 2 * core if flip else group, there)

    partner = device(0, 0, True)
    main_late = (x * (1 - core) + y * core) // 2
    side_late = (y * (1 - core) + x * core) // 2

    greeted = [device(i, 0) for i in (1, 2, 3)] + [device(0, i) for i in (1, 2, 3)]
    greeted += [partner] + [device(i, 0, True) for i in (1, 2, 3)] + [device(0, i, True) for i in (1, 2, 3)]
    barrier = pltpu.get_barrier_semaphore()
    for there in greeted:
        pl.semaphore_signal(barrier, inc=1, device_id=there, device_id_type=MESH)

    def load(c):
        at = pl.ds(c * CHUNK, CHUNK)
        return pltpu.make_async_copy(rows_hbm.at[at], blocks.at[0, at], load_sem.at[c])

    for c in range(CHUNKS):
        load(c).start()

    def normalise(c):
        load(c).wait()

        @pl.loop(0, CHUNK // 16)
        def _(i):
            at = pl.ds(pl.multiple_of(c * CHUNK + i * 16, 16), 16)
            values = blocks[0, at, :].astype(jnp.float32)
            squares = jnp.sum(values * values, axis=1, keepdims=True)
            blocks[0, at, :] = (values * lax.rsqrt(squares + 1e-06)).astype(jnp.bfloat16)

    def move(source, slot, c, there):
        at = pl.ds(c * CHUNK, CHUNK)
        return pltpu.make_async_remote_copy(
            blocks.at[source, at], blocks.at[slot, at], send_sem.at[slot, c], recv_sem.at[slot, c],
            device_id=there, device_id_type=MESH,
        )

    sent = []

    def send(source, slot, c, there):
        copy = move(source, slot, c, there)
        copy.start()
        sent.append(copy)

    def await_chunk(slot, c):
        move(slot, slot, c, partner).wait_recv()

    down, up, side_up = device(-1, 0), device(1, 0), device(0, 1)

    normalise(0)
    pl.semaphore_wait(barrier, len(greeted))
    rank_to = [(i, device(-i, 0)) for i in (1, 2, 3)] + [(NEAR, side_up), (FAR, device(0, 2))]
    rank_to += [(OTHER + i, device(-i, 0, True)) for i in range(4)]

    def rank_copy(slot, there):
        return pltpu.make_async_remote_copy(
            rank_lane.at[0], rank_lane.at[slot], rank_send.at[slot], rank_recv.at[slot], device_id=there, device_id_type=MESH
        )

    rank_lane[0] = rank_ref[...]
    for c in range(CHUNKS):
        if c:
            normalise(c)
        send(0, 1, c, down)
        send(0, NEAR, c, side_up)
        if c >= CHUNKS // 2:
            send(0, 3, c, up)
        send(0, OTHER, c, partner)
        if c == 0:
            for slot, there in rank_to:
                rank_copy(slot, there).start()

    best_row[...] = jnp.full_like(best_row, -1.0)
    best_lane[...] = jnp.full_like(best_lane, -1.0)

    def column(slot):
        for h in range(2):
            wide = jnp.broadcast_to(rank_lane[slot, h][:1], (HALF, HALF))
            rank_row[slot, pl.ds(h * HALF, HALF), :] = wide.T

    column(0)
    for slot, there in rank_to:
        rank_copy(slot, there).wait_recv()
    for slot, there in rank_to:
        column(slot)

    def meet(a, start, count, b, half, halves, both=True):
        left = blocks[a, pl.ds(start, count), :]
        right = blocks[b, pl.ds(pl.multiple_of(half * HALF, HALF), halves * HALF), :]
        scores = lax.dot_general(left, right, (((1,), (1,)), ((), ())), preferred_element_type=jnp.float32)
        mine = rank_row[a, pl.ds(start, count), :].reshape(count // 8, 8, HALF)
        best = best_row[a, pl.ds(start, count), :].reshape(count // 8, 8, HALF)
        for h in range(halves):
            part = scores[:, h * HALF : (h + 1) * HALF].reshape(count // 8, 8, HALF)
            earlier = rank_lane[b, half + h][None] < mine
            best = jnp.maximum(best, jnp.where(earlier, part, -1.0))
            if both:
                back = jnp.max(jnp.where(earlier, -1.0, part), axis=0)
                best_lane[b, half + h] = jnp.maximum(best_lane[b, half + h], back)
        best_row[a, pl.ds(start, count), :] = best.reshape(count, HALF)

    def meet_each(a, start, count, first, last):
        @pl.loop(first, last)
        def _(b):
            meet(a, start, count, b, 0, 2)

    def quarter(a, h, b, swap):
        meet(a, h * HALF, HALF, b, h + swap - 2 * h * swap, 1)

    def crossed(a, swap):
        quarter(a, 0, a + OTHER, swap)
        quarter(a, 1, a + OTHER, swap)

    def await_main(k):
        slot, c = 1 + k // CHUNKS, k % CHUNKS
        await_chunk(slot, c)
        if k < CHUNKS + CHUNKS // 2:
            send(slot, slot + 1, c, down)
        send(slot, slot + OTHER, c, partner)

    def await_side(k):
        slot, c = NEAR + k // CHUNKS, k % CHUNKS
        await_chunk(slot, c)
        if k < CHUNKS:
            send(slot, FAR, c, side_up)

    def await_other(slot, first=0, last=CHUNKS):
        for c in range(first, last):
            await_chunk(OTHER + slot, c)

    @pl.loop(0, 2)
    def _(h):
        meet(0, pl.multiple_of(h * HALF, HALF), HALF, 0, 0, 2, both=False)

    await_main(0)
    await_other(0)
    crossed(0, core)
    await_main(1)
    for b in (0, OTHER):
        meet(1, 0, HALF, b, 0, 2)
    await_main(2)
    await_side(0)
    await_main(3)
    await_side(1)
    for b in (0, OTHER):
        meet(1, HALF, HALF, b, 0, 2)
    meet_each(NEAR, 0, HALF, 0, 2)
    await_main(4)
    await_side(2)
    await_chunk(3, 2)
    send(3, 3 + OTHER, 2, partner)
    await_other(1)
    crossed(1, core)
    await_main(5)
    await_side(3)
    await_chunk(3, 3)
    send(3, 3 + OTHER, 3, partner)
    meet_each(NEAR, HALF, HALF, 0, 2)
    meet_each(2, 0, HALF, OTHER, OTHER + 2)
    quarter(2, 0, 0, main_late)
    await_main(6)
    await_side(4)
    meet(2, 0, HALF, NEAR, 0, 2)
    meet_each(3, HALF, HALF, OTHER, OTHER + 2)
    meet(3, HALF, HALF, NEAR, 0, 2)
    await_main(7)
    await_side(5)
    meet_each(2, HALF, HALF, OTHER, OTHER + 2)
    quarter(2, 1, 0, main_late)
    meet(2, HALF, HALF, NEAR, 0, 2)
    await_main(8)
    await_side(6)

    @pl.loop(0, 3)
    def _(b):
        quarter(FAR, 0, b, side_late)

    await_other(2)
    crossed(2, core)
    meet(3, HALF, HALF, OTHER + 2, 0, 2)
    meet_each(3, 0, CHUNK, OTHER, OTHER + 3)
    meet(3, 0, CHUNK, NEAR, 0, 2)
    await_main(9)
    await_side(7)
    meet_each(3, CHUNK, CHUNK, OTHER, OTHER + 3)
    meet(3, CHUNK, CHUNK, NEAR, 0, 2)

    @pl.loop(0, 3)
    def _(b):
        quarter(FAR, 1, b, side_late)

    quarter(FAR, 0, 3, side_late)
    quarter(FAR, 1, 3, side_late)
    await_other(3)
    crossed(3, core)

    def finish(slot):
        for h in range(2):
            turned = best_row[slot, pl.ds(h * HALF, HALF), :].T
            found = jnp.max(turned.reshape(HALF // 8, 8, HALF), axis=0)
            mail[slot, h] = jnp.maximum(found, best_lane[slot, h])

    owners = [(i, device(i, 0)) for i in (1, 2, 3)] + [(NEAR, device(0, -1)), (FAR, device(0, -2))]
    owners += [(OTHER + i, device(0, i, True)) for i in range(4)]

    def mail_copy(slot, there):
        return pltpu.make_async_remote_copy(
            mail.at[slot], mail.at[SLOTS + slot], mail_send.at[slot], mail_recv.at[slot], device_id=there, device_id_type=MESH
        )

    for slot, there in owners:
        finish(slot)
        mail_copy(slot, there).start()
    finish(0)
    found = mail[0]
    for slot, there in owners:
        mail_copy(slot, there).wait_recv()
        found = jnp.maximum(found, mail[SLOTS + slot])
    found = jnp.max(found, axis=1)
    out_ref[...] = jnp.where(rank_ref[:, 0, :] < EMPTY, found, -1.0)

    for copy in sent:
        copy.wait_send()
    for slot, there in rank_to:
        rank_copy(slot, there).wait_send()
    for slot, there in owners:
        mail_copy(slot, there).wait_send()


def shards(embeddings, member_order, member_count):
    rows, depth = embeddings.shape
    group, place = lax.axis_index("grp"), lax.axis_index("row")
    base = (group % 2) * lax.axis_size("row") * rows + place * rows
    live = base + jnp.arange(rows, dtype=jnp.int32) < member_count[group // 2]
    rank = jnp.where(live, member_order, EMPTY).reshape(2, 1, HALF)
    rank = jnp.broadcast_to(rank, (2, 8, HALF))
    copies = [pltpu.SemaphoreType.DMA((SLOTS, CHUNKS))] * 2
    letters = [pltpu.SemaphoreType.DMA((SLOTS,))] * 4
    best = pl.pallas_call(
        kernel,
        out_shape=jax.ShapeDtypeStruct((2, HALF), jnp.float32),
        in_specs=[pl.BlockSpec(memory_space=pl.ANY), pl.BlockSpec(memory_space=pltpu.VMEM)],
        out_specs=pl.BlockSpec(memory_space=pltpu.VMEM),
        scratch_shapes=[
            pltpu.VMEM((SLOTS, rows, depth), jnp.bfloat16),
            pltpu.VMEM((SLOTS, 2, 8, HALF), jnp.int32),
            pltpu.VMEM((SLOTS, rows, HALF), jnp.int32),
            pltpu.VMEM((SLOTS, rows, HALF), jnp.float32),
            pltpu.VMEM((SLOTS, 2, 8, HALF), jnp.float32),
            pltpu.VMEM((2 * SLOTS, 2, 8, HALF), jnp.float32),
            pltpu.SemaphoreType.DMA((CHUNKS,)),
            *copies,
            *letters,
        ],
        compiler_params=pltpu.CompilerParams(collective_id=0, has_side_effects=True, vmem_limit_bytes=48 * 2**20),
        name="nearest_earlier",
    )(embeddings, rank)
    return best.reshape(rows)


def solution(mesh):
    in_specs = (P(("grp", "row"), None), P(("grp", "row")), P())
    out_specs = P(("grp", "row"))
    return jax.shard_map(shards, mesh=mesh, in_specs=in_specs, out_specs=out_specs, check_vma=False)
```

```python
import jax
import jax.numpy as jnp
from jax import lax
from jax.experimental import pallas as pl
from jax.experimental.pallas import tpu as pltpu
from jax.sharding import PartitionSpec as P

MESH = pl.DeviceIdType.MESH
SIDE = 4
ROWS = 256
HALF = ROWS // 2
CHUNK = 64
CHUNKS = ROWS // CHUNK
ORDER = (2, 3, 0, 1)
EMPTY = 1 << 20
OTHER, NEAR, OTHER_LAST, FAR = 4, 7, 8, 9
SLOTS = 10
OTHERS = (OTHER, OTHER + 1, OTHER + 2, OTHER_LAST)
TURNED = 9 * HALF


def kernel(
    rows_hbm, order_hbm, count_hbm, out_ref, blocks, turned, turned_line, order, count, rank_lane, rank_row, best_row,
    best_lane, mail, load_sem, word_sem, send_sem, recv_sem, rank_send, rank_recv, mail_send, mail_recv,
):
    group, place = lax.axis_index("grp"), lax.axis_index("row")
    core = lax.rem(group, 2)
    x, y = place // SIDE, lax.rem(place, SIDE)

    def device(main, side, flip=False):
        dx = main * (1 - core) + side * core
        dy = main * core + side * (1 - core)
        there = lax.rem(x + dx + SIDE, SIDE) * SIDE + lax.rem(y + dy + SIDE, SIDE)
        return (group + 1 - 2 * core if flip else group, there)

    partner = device(0, 0, True)

    greeted = [device(i, 0) for i in (1, 2, 3)] + [device(0, i) for i in (1, 2, 3)]
    greeted += [partner] + [device(i, 0, True) for i in (1, 2, 3)] + [device(0, i, True) for i in (1, 2, 3)]
    barrier = pltpu.get_barrier_semaphore()
    for there in greeted:
        pl.semaphore_signal(barrier, inc=1, device_id=there, device_id_type=MESH)

    def load(c):
        at = pl.ds(c * CHUNK, CHUNK)
        return pltpu.make_async_copy(rows_hbm.at[at], blocks.at[0, at], load_sem.at[c])

    for c in ORDER:
        load(c).start()
    words = [
        pltpu.make_async_copy(order_hbm, order, word_sem.at[0]),
        pltpu.make_async_copy(count_hbm, count, word_sem.at[1]),
    ]
    for copy in words:
        copy.start()

    def normalise(c):
        load(c).wait()

        @pl.loop(0, CHUNK // 16)
        def _(i):
            at = pl.ds(pl.multiple_of(c * CHUNK + i * 16, 16), 16)
            values = blocks[0, at, :].astype(jnp.float32)
            squares = jnp.sum(values * values, axis=1, keepdims=True)
            blocks[0, at, :] = (values * lax.rsqrt(squares + 1e-06)).astype(jnp.bfloat16)

    def move(source, slot, c, there):
        at = pl.ds(c * CHUNK, CHUNK)
        return pltpu.make_async_remote_copy(
            blocks.at[source, at], blocks.at[slot, at], send_sem.at[slot, c], recv_sem.at[slot, c],
            device_id=there, device_id_type=MESH,
        )

    sent = []

    def send(source, slot, c, there):
        copy = move(source, slot, c, there)
        copy.start()
        sent.append(copy)

    def await_chunk(slot, c):
        move(slot, slot, c, partner).wait_recv()

    down, up, side_up = device(-1, 0), device(1, 0), device(0, 1)

    rank_to = [(i, device(-i, 0)) for i in (1, 2, 3)] + [(NEAR, side_up), (FAR, device(0, 2))]
    rank_to += [(OTHERS[i], device(-i, 0, True)) for i in range(4)]

    def pair(slot):
        return pl.ds(2 * slot, 2)

    def rank_copy(slot, there):
        return pltpu.make_async_remote_copy(
            rank_lane.at[pair(0)], rank_lane.at[pair(slot)], rank_send.at[slot], rank_recv.at[slot],
            device_id=there, device_id_type=MESH,
        )

    normalise(ORDER[0])
    for copy in words:
        copy.wait()
    slots = (core * SIDE * SIDE + place) * ROWS
    slots += lax.broadcasted_iota(jnp.int32, (2, HALF), 0) * HALF + lax.broadcasted_iota(jnp.int32, (2, HALF), 1)
    live = slots < count[group // 2]
    rank = jnp.where(live, order[...], EMPTY)
    rank_lane[pair(0)] = jnp.broadcast_to(rank[:, None, :], (2, 8, HALF))
    pl.semaphore_wait(barrier, len(greeted))
    for k, c in enumerate(ORDER):
        if k:
            normalise(c)
        send(0, 1, c, down)
        send(0, NEAR, c, side_up)
        if k >= CHUNKS // 2:
            send(0, 3, c, up)
        send(0, OTHER, c, partner)
        if k == 0:
            for slot, there in rank_to:
                rank_copy(slot, there).start()

    best_row[...] = jnp.full_like(best_row, -1.0)
    best_lane[...] = jnp.full_like(best_lane, -1.0)

    def column(slot):
        for h in range(2):
            wide = jnp.broadcast_to(rank_lane[2 * slot + h][:1], (HALF, HALF))
            rank_row[slot, pl.ds(h * HALF, HALF), :] = wide.T

    def turn(slot, into, first, rows=ROWS):
        @pl.loop(0, blocks.shape[2] // 256)
        def _(i):
            at = pl.ds(pl.multiple_of(i * 256, 256), 256)
            into[at, pl.ds(first, rows)] = blocks[slot, pl.ds(0, rows), at].T

    def reduce(scores, a, start, halves, both=True):
        rows = scores.shape[0]
        mine = rank_row[a, pl.ds(start, rows), :].reshape(rows // 8, 8, HALF)
        best = best_row[a, pl.ds(start, rows), :].reshape(rows // 8, 8, HALF)
        for i, half in enumerate(halves):
            part = scores[:, i * HALF : (i + 1) * HALF].reshape(rows // 8, 8, HALF)
            earlier = rank_lane[half][None] < mine
            best = jnp.maximum(best, jnp.where(earlier, part, -1.0))
            if both:
                best_lane[half] = jnp.maximum(best_lane[half], jnp.max(jnp.where(earlier, -1.0, part), axis=0))
        best_row[a, pl.ds(start, rows), :] = best.reshape(rows, HALF)

    def meet(a, b, start=0, rows=ROWS, other=0, other_rows=ROWS, both=True):
        left, right = blocks[a, pl.ds(start, rows), :], blocks[b, pl.ds(other, other_rows), :]
        scores = lax.dot_general(left, right, (((1,), (1,)), ((), ())), preferred_element_type=jnp.float32)
        first = 2 * b + other // HALF
        reduce(scores, a, start, [first + i for i in range(other_rows // HALF)], both)

    def meet_turned(a, start, rows, columns, first, count, half):
        scores = jnp.dot(
            blocks[a, pl.ds(start, rows), :], columns[:, pl.ds(first, count)], preferred_element_type=jnp.float32
        )
        reduce(scores, a, start, [half + i for i in range(count // HALF)])

    def meet_others(a, first, last):
        @pl.loop(first, last)
        def _(i):
            meet_turned(a, 0, ROWS, turned, pl.multiple_of(i * ROWS, ROWS), ROWS, 2 * OTHER + 2 * i)

    def fold(slot, halves=(0, 1)):
        for h in halves:
            flat = best_row[slot, pl.ds(h * HALF, HALF), :].T
            found = jnp.max(flat.reshape(HALF // 8, 8, HALF), axis=0)
            best_lane[2 * slot + h] = jnp.maximum(best_lane[2 * slot + h], found)

    def await_main(k):
        slot, c = 1 + k // CHUNKS, ORDER[k % CHUNKS]
        await_chunk(slot, c)
        if k < CHUNKS + CHUNKS // 2:
            send(slot, slot + 1, c, down)
        send(slot, OTHERS[slot], c, partner)

    def await_side(k):
        slot, c = (NEAR, FAR)[k // CHUNKS], ORDER[k % CHUNKS]
        await_chunk(slot, c)
        if k < CHUNKS:
            send(slot, FAR, c, side_up)

    def await_up(k):
        await_chunk(3, k)
        send(3, OTHER_LAST, k, partner)

    def await_other(slot, chunks=ORDER):
        for c in chunks:
            await_chunk(slot, c)

    column(0)
    meet(0, 0, both=False)
    turn(0, turned_line, 0)
    await_main(0)
    for slot, there in rank_to:
        rank_copy(slot, there).wait_recv()
    for slot in (1, 2, 3, FAR):
        column(slot)
    await_other(OTHER)
    turn(OTHER, turned, 0)
    meet_others(0, 0, 1)
    await_main(1)
    await_main(2)
    await_side(0)
    await_main(3)
    await_side(1)
    meet_turned(1, 0, ROWS, turned_line, 0, ROWS, 0)
    meet_others(1, 0, 1)
    turn(1, turned_line, ROWS)
    await_main(4)
    await_side(2)
    await_up(0)
    await_other(OTHER + 1)
    turn(OTHER + 1, turned, ROWS)
    meet_others(1, 1, 2)
    await_main(5)
    await_side(3)
    await_up(1)
    turn(NEAR, turned, 3 * ROWS)
    meet_others(0, 3, 4)
    meet_others(1, 3, 4)
    await_main(6)
    await_side(4)
    await_other(OTHER_LAST, ORDER[2:])
    turn(OTHER_LAST, turned, 4 * ROWS, HALF)
    await_main(7)
    await_side(5)
    meet_others(2, 0, 2)
    meet_others(2, 3, 4)
    meet_turned(2, 0, ROWS, turned_line, 0, ROWS, 0)
    turn(2, turned_line, 2 * ROWS)
    await_main(8)
    await_side(6)
    await_other(OTHER + 2)
    turn(OTHER + 2, turned, 2 * ROWS)
    meet_others(2, 2, 3)
    for slot in (0, 1, 2):
        fold(slot)

    owners = [(i, device(i, 0)) for i in (1, 2, 3)] + [(NEAR, device(0, -1)), (FAR, device(0, -2))]
    owners += [(OTHERS[i], device(0, i, True)) for i in range(4)]

    def mail_copy(slot, there):
        return pltpu.make_async_remote_copy(
            best_lane.at[pair(slot)], mail.at[pair(slot)], mail_send.at[slot], mail_recv.at[slot],
            device_id=there, device_id_type=MESH,
        )

    def post(*slots):
        for slot, there in owners:
            if slot in slots:
                mail_copy(slot, there).start()

    meet_turned(3, 0, HALF, turned, 0, TURNED, 2 * OTHER)
    meet_turned(FAR, HALF, HALF, turned_line, 0, 3 * ROWS, 0)
    fold(3, (0,))
    fold(FAR, (1,))
    await_main(9)
    await_side(7)
    meet_turned(3, HALF, HALF, turned, 0, TURNED, 2 * OTHER)
    post(OTHER, OTHER + 1, OTHER + 2, NEAR)
    meet_turned(FAR, 0, HALF, turned_line, 0, 3 * ROWS, 0)
    post(1, 2)
    fold(FAR, (0,))
    post(FAR)
    await_other(OTHER_LAST, ORDER[:2])
    meet(3, OTHER_LAST, HALF, HALF, HALF, HALF)
    post(OTHER_LAST)
    fold(3, (1,))
    post(3)

    found = best_lane[pair(0)]
    for slot, there in owners:
        mail_copy(slot, there).wait_recv()
        found = jnp.maximum(found, mail[pair(slot)])
    out_ref[...] = jnp.where(rank_lane[pair(0)][:, 0, :] < EMPTY, jnp.max(found, axis=1), -1.0)

    for copy in sent:
        copy.wait_send()
    for slot, there in rank_to:
        rank_copy(slot, there).wait_send()
    for slot, there in owners:
        mail_copy(slot, there).wait_send()


def shards(embeddings, member_order, member_count):
    rows, depth = embeddings.shape
    copies = [pltpu.SemaphoreType.DMA((SLOTS, CHUNKS))] * 2
    letters = [pltpu.SemaphoreType.DMA((SLOTS,))] * 4
    best = pl.pallas_call(
        kernel,
        out_shape=jax.ShapeDtypeStruct((2, HALF), jnp.float32),
        in_specs=[pl.BlockSpec(memory_space=pltpu.HBM)] * 3,
        out_specs=pl.BlockSpec(memory_space=pltpu.VMEM),
        scratch_shapes=[
            pltpu.VMEM((SLOTS, rows, depth), jnp.bfloat16),
            pltpu.VMEM((depth, TURNED), jnp.bfloat16),
            pltpu.VMEM((depth, 3 * rows), jnp.bfloat16),
            pltpu.VMEM((2, HALF), jnp.int32),
            pltpu.SMEM(member_count.shape, jnp.int32),
            pltpu.VMEM((2 * SLOTS, 8, HALF), jnp.int32),
            pltpu.VMEM((SLOTS, rows, HALF), jnp.int32),
            pltpu.VMEM((SLOTS, rows, HALF), jnp.float32),
            pltpu.VMEM((2 * SLOTS, 8, HALF), jnp.float32),
            pltpu.VMEM((2 * SLOTS, 8, HALF), jnp.float32),
            pltpu.SemaphoreType.DMA((CHUNKS,)),
            pltpu.SemaphoreType.DMA((2,)),
            *copies,
            *letters,
        ],
        compiler_params=pltpu.CompilerParams(collective_id=0, has_side_effects=True, vmem_limit_bytes=60 * 2**20),
        name="nearest_earlier",
    )(embeddings, member_order.reshape(2, HALF), member_count)
    return best.reshape(rows)


def solution(mesh):
    in_specs = (P(("grp", "row"), None), P(("grp", "row")), P())
    out_specs = P(("grp", "row"))
    return jax.shard_map(shards, mesh=mesh, in_specs=in_specs, out_specs=out_specs, check_vma=False)
```

```python
import jax
import jax.numpy as jnp
from jax import lax
from jax.experimental import pallas as pl
from jax.experimental.pallas import tpu as pltpu
from jax.sharding import PartitionSpec as P

MESH = pl.DeviceIdType.MESH
SIDE = 4
ROWS = 256
HALF = ROWS // 2
CHUNK = 64
CHUNKS = ROWS // CHUNK
ORDER = (2, 3, 0, 1)
EMPTY = 1 << 20
OTHER, NEAR, OTHER_LAST, FAR, RELAY = 4, 7, 8, 9, 10
SLOTS = 11
OTHERS = (OTHER, OTHER + 1, OTHER + 2, OTHER_LAST)
TURNED = 4 * ROWS


def kernel(
    rows_hbm, order_hbm, count_hbm, out_ref, blocks, turned, turned_own, order, count, rank_lane, rank_row, best_row,
    best_lane, mail, load_sem, word_sem, send_sem, recv_sem, rank_send, rank_recv, mail_send, mail_recv,
):
    group, place = lax.axis_index("grp"), lax.axis_index("row")
    core = lax.rem(group, 2)
    x, y = place // SIDE, lax.rem(place, SIDE)

    def device(main, side, flip=False):
        dx = main * (1 - core) + side * core
        dy = main * core + side * (1 - core)
        there = lax.rem(x + dx + SIDE, SIDE) * SIDE + lax.rem(y + dy + SIDE, SIDE)
        return (group + 1 - 2 * core if flip else group, there)

    partner = device(0, 0, True)
    parity = lax.rem(group // 2, 2)
    step = 1 - 2 * lax.rem(parity + core, 2)
    across = (lax.rem(group // 2 + step + SIDE, SIDE) * 2 + core, place)
    along = x * core + y * (1 - core)
    near_goes_on = lax.rem(along + 3, SIDE) // 2 == parity
    far_here = lax.rem(along + 2, SIDE) // 2 == parity

    greeted = [device(i, 0) for i in (1, 2, 3)] + [device(0, i) for i in (1, 2, 3)]
    greeted += [partner, across] + [device(i, 0, True) for i in (1, 2, 3)] + [device(0, i, True) for i in (1, 2, 3)]
    barrier = pltpu.get_barrier_semaphore()
    for there in greeted:
        pl.semaphore_signal(barrier, inc=1, device_id=there, device_id_type=MESH)

    def load(c):
        at = pl.ds(c * CHUNK, CHUNK)
        return pltpu.make_async_copy(rows_hbm.at[at], blocks.at[0, at], load_sem.at[c])

    for c in ORDER:
        load(c).start()
    words = [
        pltpu.make_async_copy(order_hbm, order, word_sem.at[0]),
        pltpu.make_async_copy(count_hbm, count, word_sem.at[1]),
    ]
    for copy in words:
        copy.start()

    def normalise(c):
        load(c).wait()

        @pl.loop(0, CHUNK // 16)
        def _(i):
            at = pl.ds(pl.multiple_of(c * CHUNK + i * 16, 16), 16)
            values = blocks[0, at, :].astype(jnp.float32)
            squares = jnp.sum(values * values, axis=1, keepdims=True)
            blocks[0, at, :] = (values * lax.rsqrt(squares + 1e-06)).astype(jnp.bfloat16)

    def move(source, slot, c, there, leaves=None):
        at = pl.ds(c * CHUNK, CHUNK)
        return pltpu.make_async_remote_copy(
            blocks.at[source, at], blocks.at[slot, at], leaves or send_sem.at[slot, c], recv_sem.at[slot, c],
            device_id=there, device_id_type=MESH,
        )

    sent = []

    def send(source, slot, c, there):
        copy = move(source, slot, c, there)
        copy.start()
        sent.append(copy)

    def direct(c):
        return move(NEAR, FAR, c, side_up)

    def out(c):
        return move(NEAR, RELAY, c, across)

    def relayed(c):
        return move(RELAY, FAR, c, side_up)

    def back(c):
        return move(FAR, FAR, c, across, send_sem.at[RELAY, c - CHUNKS // 2])

    def await_chunk(slot, c):
        move(slot, slot, c, partner).wait_recv()

    down, up, side_up = device(-1, 0), device(1, 0), device(0, 1)

    rank_to = [(i, device(-i, 0)) for i in (1, 2, 3)] + [(NEAR, side_up), (FAR, device(0, 2))]
    rank_to += [(OTHERS[i], device(-i, 0, True)) for i in range(4)]

    def pair(slot):
        return pl.ds(2 * slot, 2)

    def rank_copy(slot, there):
        return pltpu.make_async_remote_copy(
            rank_lane.at[pair(0)], rank_lane.at[pair(slot)], rank_send.at[slot], rank_recv.at[slot],
            device_id=there, device_id_type=MESH,
        )

    normalise(ORDER[0])
    for copy in words:
        copy.wait()
    slots = (core * SIDE * SIDE + place) * ROWS
    slots += lax.broadcasted_iota(jnp.int32, (2, HALF), 0) * HALF + lax.broadcasted_iota(jnp.int32, (2, HALF), 1)
    live = slots < count[group // 2]
    rank = jnp.where(live, order[...], EMPTY)
    rank_lane[pair(0)] = jnp.broadcast_to(rank[:, None, :], (2, 8, HALF))
    pl.semaphore_wait(barrier, len(greeted))
    for k, c in enumerate(ORDER):
        if k:
            normalise(c)
        send(0, 1, c, down)
        send(0, NEAR, c, side_up)
        send(0, OTHER, c, partner)
        if k == 0:
            for slot, there in rank_to:
                rank_copy(slot, there).start()

    best_row[...] = jnp.full_like(best_row, -1.0)
    best_lane[...] = jnp.full_like(best_lane, -1.0)

    def column(slot):
        for h in range(2):
            wide = jnp.broadcast_to(rank_lane[2 * slot + h][:1], (HALF, HALF))
            rank_row[slot, pl.ds(h * HALF, HALF), :] = wide.T

    def turn(slot, into, first, start=0, rows=ROWS):
        @pl.loop(0, blocks.shape[2] // 256)
        def _(i):
            at = pl.ds(pl.multiple_of(i * 256, 256), 256)
            into[at, pl.ds(first, rows)] = blocks[slot, pl.ds(start, rows), at].T

    def reduce(scores, a, start, halves, both=True):
        rows = scores.shape[0]
        mine = rank_row[a, pl.ds(start, rows), :].reshape(rows // 8, 8, HALF)
        best = best_row[a, pl.ds(start, rows), :].reshape(rows // 8, 8, HALF)
        for i, half in enumerate(halves):
            part = scores[:, i * HALF : (i + 1) * HALF].reshape(rows // 8, 8, HALF)
            earlier = rank_lane[half][None] < mine
            best = jnp.maximum(best, jnp.where(earlier, part, -1.0))
            if both:
                best_lane[half] = jnp.maximum(best_lane[half], jnp.max(jnp.where(earlier, -1.0, part), axis=0))
        best_row[a, pl.ds(start, rows), :] = best.reshape(rows, HALF)

    def meet(a, b, start=0, rows=ROWS, other=0, other_rows=ROWS, both=True):
        left, right = blocks[a, pl.ds(start, rows), :], blocks[b, pl.ds(other, other_rows), :]
        scores = lax.dot_general(left, right, (((1,), (1,)), ((), ())), preferred_element_type=jnp.float32)
        first = 2 * b + other // HALF
        reduce(scores, a, start, [first + i for i in range(other_rows // HALF)], both)

    def meet_turned(a, start, rows, columns, first, count, half):
        scores = jnp.dot(
            blocks[a, pl.ds(start, rows), :], columns[:, pl.ds(first, count)], preferred_element_type=jnp.float32
        )
        reduce(scores, a, start, [half + i for i in range(count // HALF)])

    def meet_others(a, first, last):
        @pl.loop(first, last)
        def _(i):
            meet_turned(a, 0, ROWS, turned, pl.multiple_of(i * ROWS, ROWS), ROWS, 2 * OTHER + 2 * i)

    def fold(slot, halves=(0, 1)):
        for h in halves:
            flat = best_row[slot, pl.ds(h * HALF, HALF), :].T
            found = jnp.max(flat.reshape(HALF // 8, 8, HALF), axis=0)
            best_lane[2 * slot + h] = jnp.maximum(best_lane[2 * slot + h], found)

    def await_main(k):
        slot, c = 1 + k // CHUNKS, ORDER[k % CHUNKS]
        await_chunk(slot, c)
        if k <= CHUNKS:
            send(slot, slot + 1, c, down)
        send(slot, OTHERS[slot], c, partner)
        if k == 5:
            for c in ORDER[2:] + ORDER[1:2]:
                send(0, 3, c, up)

    def await_near(c):
        await_chunk(NEAR, c)

        @pl.when(near_goes_on)
        def _():
            (direct if c in ORDER[2:] else out)(c).start()

    def await_relay(c):
        @pl.when(jnp.logical_not(near_goes_on))
        def _():
            await_chunk(RELAY, c)
            relayed(c).start()

    def await_far(c):
        @pl.when(far_here)
        def _():
            await_chunk(FAR, c)

    def await_back(c):
        @pl.when(jnp.logical_not(far_here))
        def _():
            await_chunk(FAR, c)
            back(c).start()

    def await_up(k):
        await_chunk(3, k)
        send(3, OTHER_LAST, k, partner)

    def await_other(slot, chunks=ORDER):
        for c in chunks:
            await_chunk(slot, c)

    column(0)
    meet(0, 0, both=False)
    turn(0, turned_own, 0)
    await_main(0)
    await_near(ORDER[0])
    for slot, there in rank_to:
        rank_copy(slot, there).wait_recv()
    for slot in (1, 2, 3):
        column(slot)
    await_other(OTHER)
    turn(OTHER, turned, 0)
    meet_others(0, 0, 1)
    await_main(1)
    await_near(ORDER[1])
    await_relay(ORDER[0])
    await_main(2)
    await_near(ORDER[2])
    await_relay(ORDER[1])
    await_main(3)
    await_near(ORDER[3])
    meet_turned(1, 0, ROWS, turned_own, 0, ROWS, 0)
    meet_others(1, 0, 1)
    await_main(4)
    await_back(ORDER[0])
    await_other(OTHER + 1)
    turn(OTHER + 1, turned, ROWS)
    meet_others(1, 1, 2)
    turn(NEAR, turned, 3 * ROWS)
    await_main(5)
    await_back(ORDER[1])
    meet_others(0, 3, 4)
    meet_others(1, 3, 4)
    meet_turned(2, HALF, HALF, turned_own, 0, ROWS, 0)
    meet_turned(2, HALF, HALF, turned, 0, 2 * ROWS, 2 * OTHER)
    meet_turned(2, HALF, HALF, turned, 3 * ROWS, ROWS, 2 * NEAR)
    await_main(6)
    await_up(ORDER[2])
    await_other(OTHER + 2, ORDER[:2])
    turn(OTHER + 2, turned, 2 * ROWS + HALF, HALF, HALF)
    await_main(7)
    meet_turned(2, 0, HALF, turned_own, 0, HALF, 0)
    meet_turned(2, 0, HALF, turned, 0, 2 * ROWS, 2 * OTHER)
    meet_turned(2, 0, HALF, turned, 3 * ROWS, ROWS, 2 * NEAR)
    await_other(OTHER + 2, ORDER[2:])
    turn(OTHER + 2, turned, 2 * ROWS, 0, HALF)
    meet_others(2, 2, 3)
    await_up(ORDER[3])
    meet_turned(3, 0, HALF, turned, 0, TURNED, 2 * OTHER)
    for c in ORDER:
        await_far(c)

    @pl.when(far_here)
    def _():
        @pl.loop(0, 3)
        def _(a):
            meet(a, FAR)

    for slot in (0, 1, 2):
        fold(slot)

    owners = [(i, device(i, 0)) for i in (1, 2, 3)] + [(NEAR, device(0, -1)), (FAR, device(0, -2))]
    owners += [(OTHERS[i], device(0, i, True)) for i in range(4)]

    def mail_copy(slot, there):
        return pltpu.make_async_remote_copy(
            best_lane.at[pair(slot)], mail.at[pair(slot)], mail_send.at[slot], mail_recv.at[slot],
            device_id=there, device_id_type=MESH,
        )

    def post(*slots):
        for slot, there in owners:
            if slot in slots:
                mail_copy(slot, there).start()

    post(1, 2)
    await_main(8)
    await_up(ORDER[1])
    meet_turned(3, HALF, HALF, turned, 0, TURNED, 2 * OTHER)
    post(OTHER, OTHER + 1, OTHER + 2, NEAR)

    @pl.when(far_here)
    def _():
        meet(3, FAR)

    post(FAR)
    await_other(OTHER_LAST)
    meet(3, OTHER_LAST)
    post(OTHER_LAST)
    fold(3)
    post(3)

    found = best_lane[pair(0)]
    for slot, there in owners:
        mail_copy(slot, there).wait_recv()
        found = jnp.maximum(found, mail[pair(slot)])
    out_ref[...] = jnp.where(rank_lane[pair(0)][:, 0, :] < EMPTY, jnp.max(found, axis=1), -1.0)

    for copy in sent:
        copy.wait_send()

    @pl.when(near_goes_on)
    def _():
        for c in ORDER[:2]:
            out(c).wait_send()
        for c in ORDER[2:]:
            direct(c).wait_send()

    @pl.when(jnp.logical_not(near_goes_on))
    def _():
        for c in ORDER[:2]:
            relayed(c).wait_send()

    @pl.when(jnp.logical_not(far_here))
    def _():
        for c in ORDER[:2]:
            back(c).wait_send()

    for slot, there in rank_to:
        rank_copy(slot, there).wait_send()
    for slot, there in owners:
        mail_copy(slot, there).wait_send()


def shards(embeddings, member_order, member_count):
    rows, depth = embeddings.shape
    copies = [pltpu.SemaphoreType.DMA((SLOTS, CHUNKS))] * 2
    letters = [pltpu.SemaphoreType.DMA((SLOTS,))] * 4
    best = pl.pallas_call(
        kernel,
        out_shape=jax.ShapeDtypeStruct((2, HALF), jnp.float32),
        in_specs=[pl.BlockSpec(memory_space=pltpu.HBM)] * 3,
        out_specs=pl.BlockSpec(memory_space=pltpu.VMEM),
        scratch_shapes=[
            pltpu.VMEM((SLOTS, rows, depth), jnp.bfloat16),
            pltpu.VMEM((depth, TURNED), jnp.bfloat16),
            pltpu.VMEM((depth, rows), jnp.bfloat16),
            pltpu.VMEM((2, HALF), jnp.int32),
            pltpu.SMEM(member_count.shape, jnp.int32),
            pltpu.VMEM((2 * SLOTS, 8, HALF), jnp.int32),
            pltpu.VMEM((SLOTS, rows, HALF), jnp.int32),
            pltpu.VMEM((SLOTS, rows, HALF), jnp.float32),
            pltpu.VMEM((2 * SLOTS, 8, HALF), jnp.float32),
            pltpu.VMEM((2 * SLOTS, 8, HALF), jnp.float32),
            pltpu.SemaphoreType.DMA((CHUNKS,)),
            pltpu.SemaphoreType.DMA((2,)),
            *copies,
            *letters,
        ],
        compiler_params=pltpu.CompilerParams(collective_id=0, has_side_effects=True, vmem_limit_bytes=60 * 2**20),
        name="nearest_earlier",
    )(embeddings, member_order.reshape(2, HALF), member_count)
    return best.reshape(rows)


def solution(mesh):
    in_specs = (P(("grp", "row"), None), P(("grp", "row")), P())
    out_specs = P(("grp", "row"))
    return jax.shard_map(shards, mesh=mesh, in_specs=in_specs, out_specs=out_specs, check_vma=False)
```

```python
import jax
import jax.numpy as jnp
from jax import lax
from jax.experimental import pallas as pl
from jax.experimental.pallas import tpu as pltpu
from jax.sharding import PartitionSpec as P

MESH = pl.DeviceIdType.MESH
SIDE = 4
ROWS = 256
HALF = ROWS // 2
CHUNK = 64
CHUNKS = ROWS // CHUNK
ORDER = (2, 3, 0, 1)
EMPTY = 1 << 20
OTHER, NEAR, OTHER_LAST, FAR, RELAY = 4, 7, 8, 9, 10
SLOTS = 11
OTHERS = (OTHER, OTHER + 1, OTHER + 2, OTHER_LAST)
TURNED = 4 * ROWS


def kernel(
    rows_hbm, order_hbm, count_hbm, out_ref, blocks, turned, turned_own, order, count, rank_lane, rank_row, best_row,
    best_lane, mail, load_sem, word_sem, send_sem, recv_sem, rank_send, rank_recv, mail_send, mail_recv,
):
    group, place = lax.axis_index("grp"), lax.axis_index("row")
    core = lax.rem(group, 2)
    x, y = place // SIDE, lax.rem(place, SIDE)

    def device(main, side, flip=False):
        dx = main * (1 - core) + side * core
        dy = main * core + side * (1 - core)
        there = lax.rem(x + dx + SIDE, SIDE) * SIDE + lax.rem(y + dy + SIDE, SIDE)
        return (group + 1 - 2 * core if flip else group, there)

    partner = device(0, 0, True)
    parity = lax.rem(group // 2, 2)
    step = 1 - 2 * lax.rem(parity + core, 2)
    plane = lax.rem(group // 2 + step + SIDE, SIDE) * 2 + core
    across, ahead, behind = (plane, place), (plane, device(0, 1)[1]), (plane, device(0, -1)[1])
    along = x * core + y * (1 - core)
    near_goes_on = lax.rem(along + 3, SIDE) // 2 == parity
    far_here = lax.rem(along + 2, SIDE) // 2 == parity

    def load(c):
        at = pl.ds(c * CHUNK, CHUNK)
        return pltpu.make_async_copy(rows_hbm.at[at], blocks.at[0, at], load_sem.at[c])

    for c in ORDER:
        load(c).start()
    words = [
        pltpu.make_async_copy(order_hbm, order, word_sem.at[0]),
        pltpu.make_async_copy(count_hbm, count, word_sem.at[1]),
    ]
    for copy in words:
        copy.start()

    greeted = [device(i, 0) for i in (1, 2, 3)] + [device(0, i) for i in (1, 2, 3)]
    greeted += [partner, across, ahead, behind] + [device(i, 0, True) for i in (1, 2, 3)] + [device(0, i, True) for i in (1, 2, 3)]
    barrier = pltpu.get_barrier_semaphore()
    for there in greeted:
        pl.semaphore_signal(barrier, inc=1, device_id=there, device_id_type=MESH)

    def normalise(c):
        load(c).wait()

        @pl.loop(0, CHUNK // 16)
        def _(i):
            at = pl.ds(pl.multiple_of(c * CHUNK + i * 16, 16), 16)
            values = blocks[0, at, :].astype(jnp.float32)
            squares = jnp.sum(values * values, axis=1, keepdims=True)
            blocks[0, at, :] = (values * lax.rsqrt(squares + 1e-06)).astype(jnp.bfloat16)

    def move(source, slot, c, there):
        at = pl.ds(c * CHUNK, CHUNK)
        return pltpu.make_async_remote_copy(
            blocks.at[source, at], blocks.at[slot, at], send_sem.at[slot, c], recv_sem.at[slot, c],
            device_id=there, device_id_type=MESH,
        )

    sent = []

    def send(source, slot, c, there):
        copy = move(source, slot, c, there)
        copy.start()
        sent.append(copy)

    def direct(c):
        return move(NEAR, FAR, c, side_up)

    def out(c):
        return move(NEAR, RELAY, c, across)

    def relayed(c):
        return move(RELAY, FAR, c, ahead)

    def await_chunk(slot, c):
        move(slot, slot, c, partner).wait_recv()

    down, up, side_up = device(-1, 0), device(1, 0), device(0, 1)

    rank_to = [(i, device(-i, 0)) for i in (1, 2, 3)] + [(NEAR, side_up), (FAR, device(0, 2))]
    rank_to += [(OTHERS[i], device(-i, 0, True)) for i in range(4)]

    def pair(slot):
        return pl.ds(2 * slot, 2)

    def rank_copy(slot, there):
        return pltpu.make_async_remote_copy(
            rank_lane.at[pair(0)], rank_lane.at[pair(slot)], rank_send.at[slot], rank_recv.at[slot],
            device_id=there, device_id_type=MESH,
        )

    normalise(ORDER[0])
    for copy in words:
        copy.wait()
    slots = (core * SIDE * SIDE + place) * ROWS
    slots += lax.broadcasted_iota(jnp.int32, (2, HALF), 0) * HALF + lax.broadcasted_iota(jnp.int32, (2, HALF), 1)
    live = slots < count[group // 2]
    rank = jnp.where(live, order[...], EMPTY)
    rank_lane[pair(0)] = jnp.broadcast_to(rank[:, None, :], (2, 8, HALF))
    pl.semaphore_wait(barrier, len(greeted))
    for k, c in enumerate(ORDER):
        if k:
            normalise(c)
        send(0, 1, c, down)
        send(0, NEAR, c, side_up)
        send(0, OTHER, c, partner)
        if k == 0:
            for slot, there in rank_to:
                rank_copy(slot, there).start()

    best_row[...] = jnp.full_like(best_row, -1.0)
    best_lane[...] = jnp.full_like(best_lane, -1.0)

    def column(slot):
        for h in range(2):
            wide = jnp.broadcast_to(rank_lane[2 * slot + h][:1], (HALF, HALF))
            rank_row[slot, pl.ds(h * HALF, HALF), :] = wide.T

    def turn(slot, into, first, start=0, rows=ROWS):
        @pl.loop(0, blocks.shape[2] // 256)
        def _(i):
            at = pl.ds(pl.multiple_of(i * 256, 256), 256)
            into[at, pl.ds(first, rows)] = blocks[slot, pl.ds(start, rows), at].T

    def reduce(scores, a, start, halves, both=True):
        rows = scores.shape[0]
        mine = rank_row[a, pl.ds(start, rows), :].reshape(rows // 8, 8, HALF)
        best = best_row[a, pl.ds(start, rows), :].reshape(rows // 8, 8, HALF)
        for i, half in enumerate(halves):
            part = scores[:, i * HALF : (i + 1) * HALF].reshape(rows // 8, 8, HALF)
            earlier = rank_lane[half][None] < mine
            best = jnp.maximum(best, jnp.where(earlier, part, -1.0))
            if both:
                best_lane[half] = jnp.maximum(best_lane[half], jnp.max(jnp.where(earlier, -1.0, part), axis=0))
        best_row[a, pl.ds(start, rows), :] = best.reshape(rows, HALF)

    def meet(a, b, start=0, rows=ROWS, other=0, other_rows=ROWS, both=True):
        left, right = blocks[a, pl.ds(start, rows), :], blocks[b, pl.ds(other, other_rows), :]
        scores = lax.dot_general(left, right, (((1,), (1,)), ((), ())), preferred_element_type=jnp.float32)
        first = 2 * b + other // HALF
        reduce(scores, a, start, [first + i for i in range(other_rows // HALF)], both)

    def meet_turned(a, start, rows, columns, first, count, half):
        scores = jnp.dot(
            blocks[a, pl.ds(start, rows), :], columns[:, pl.ds(first, count)], preferred_element_type=jnp.float32
        )
        reduce(scores, a, start, [half + i for i in range(count // HALF)])

    def meet_others(a, first, last):
        @pl.loop(first, last)
        def _(i):
            meet_turned(a, 0, ROWS, turned, pl.multiple_of(i * ROWS, ROWS), ROWS, 2 * OTHER + 2 * i)

    def fold(slot, halves=(0, 1)):
        for h in halves:
            flat = best_row[slot, pl.ds(h * HALF, HALF), :].T
            found = jnp.max(flat.reshape(HALF // 8, 8, HALF), axis=0)
            best_lane[2 * slot + h] = jnp.maximum(best_lane[2 * slot + h], found)

    def await_main(k):
        slot, c = 1 + k // CHUNKS, ORDER[k % CHUNKS]
        await_chunk(slot, c)
        if k <= CHUNKS:
            send(slot, slot + 1, c, down)
        send(slot, OTHERS[slot], c, partner)
        if k == 4:
            for c in ORDER[2:] + ORDER[1:2]:
                send(0, 3, c, up)

    def await_near(c):
        await_chunk(NEAR, c)

        @pl.when(near_goes_on)
        def _():
            (direct if c in ORDER[2:] else out)(c).start()

    def await_relay(c):
        @pl.when(jnp.logical_not(near_goes_on))
        def _():
            await_chunk(RELAY, c)
            relayed(c).start()

    def await_far(c):
        @pl.when(far_here)
        def _():
            await_chunk(FAR, c)

    def await_up(k):
        await_chunk(3, k)
        send(3, OTHER_LAST, k, partner)

    def await_other(slot, chunks=ORDER):
        for c in chunks:
            await_chunk(slot, c)

    column(0)
    meet(0, 0, both=False)
    turn(0, turned_own, 0)
    await_main(0)
    await_near(ORDER[0])
    for slot, there in rank_to:
        rank_copy(slot, there).wait_recv()
    for slot in (1, 2, 3):
        column(slot)
    await_other(OTHER)
    turn(OTHER, turned, 0)
    meet_others(0, 0, 1)
    await_main(1)
    await_near(ORDER[1])
    await_relay(ORDER[0])
    await_main(2)
    await_near(ORDER[2])
    await_relay(ORDER[1])
    await_main(3)
    await_near(ORDER[3])
    meet_turned(1, 0, ROWS, turned_own, 0, ROWS, 0)
    meet_others(1, 0, 1)
    await_main(4)
    await_other(OTHER + 1)
    turn(OTHER + 1, turned, ROWS)
    meet_others(1, 1, 2)
    turn(NEAR, turned, 3 * ROWS)
    await_main(5)
    meet_others(0, 3, 4)
    meet_others(1, 3, 4)
    meet_turned(2, HALF, HALF, turned_own, 0, ROWS, 0)
    meet_turned(2, HALF, HALF, turned, 0, 2 * ROWS, 2 * OTHER)
    meet_turned(2, HALF, HALF, turned, 3 * ROWS, ROWS, 2 * NEAR)
    await_main(6)
    await_up(ORDER[2])
    await_other(OTHER + 2, ORDER[:2])
    turn(OTHER + 2, turned, 2 * ROWS + HALF, HALF, HALF)
    for c in ORDER:
        await_far(c)

    @pl.when(far_here)
    def _():
        @pl.loop(0, 2)
        def _(a):
            meet(a, FAR)

    await_main(7)
    meet_turned(2, 0, HALF, turned_own, 0, HALF, 0)
    meet_turned(2, 0, HALF, turned, 0, 2 * ROWS, 2 * OTHER)
    meet_turned(2, 0, HALF, turned, 3 * ROWS, ROWS, 2 * NEAR)
    await_other(OTHER + 2, ORDER[2:])
    turn(OTHER + 2, turned, 2 * ROWS, 0, HALF)
    meet_others(2, 2, 3)
    await_up(ORDER[3])

    @pl.when(far_here)
    def _():
        meet(2, FAR)

    meet_turned(3, 0, HALF, turned, 0, TURNED, 2 * OTHER)
    for slot in (0, 1, 2):
        fold(slot)

    owners = [(i, device(i, 0)) for i in (1, 2, 3)] + [(NEAR, device(0, -1)), (FAR, device(0, -2))]
    owners += [(OTHERS[i], device(0, i, True)) for i in range(4)]

    def mail_copy(slot, there):
        return pltpu.make_async_remote_copy(
            best_lane.at[pair(slot)], mail.at[pair(slot)], mail_send.at[slot], mail_recv.at[slot],
            device_id=there, device_id_type=MESH,
        )

    def post(*slots):
        for slot, there in owners:
            if slot in slots:
                mail_copy(slot, there).start()

    post(1, 2)
    await_main(8)
    await_up(ORDER[1])
    meet_turned(3, HALF, HALF, turned, 0, TURNED, 2 * OTHER)
    post(OTHER, OTHER + 1, OTHER + 2, NEAR)

    @pl.when(far_here)
    def _():
        meet(3, FAR)

    post(FAR)
    await_other(OTHER_LAST, ORDER[2:])
    meet(3, OTHER_LAST, other_rows=HALF)
    fold(3, (0,))
    await_other(OTHER_LAST, ORDER[:2])
    meet(3, OTHER_LAST, HALF, HALF, HALF, HALF)
    post(OTHER_LAST)
    fold(3, (1,))
    post(3)

    for copy in sent:
        copy.wait_send()

    @pl.when(near_goes_on)
    def _():
        for c in ORDER[:2]:
            out(c).wait_send()
        for c in ORDER[2:]:
            direct(c).wait_send()

    @pl.when(jnp.logical_not(near_goes_on))
    def _():
        for c in ORDER[:2]:
            relayed(c).wait_send()

    for slot, there in rank_to:
        rank_copy(slot, there).wait_send()

    found = best_lane[pair(0)]
    for slot, there in owners:
        mail_copy(slot, there).wait_recv()
        found = jnp.maximum(found, mail[pair(slot)])
    out_ref[...] = jnp.where(rank_lane[pair(0)][:, 0, :] < EMPTY, jnp.max(found, axis=1), -1.0)

    for slot, there in owners:
        mail_copy(slot, there).wait_send()


def shards(embeddings, member_order, member_count):
    rows, depth = embeddings.shape
    copies = [pltpu.SemaphoreType.DMA((SLOTS, CHUNKS))] * 2
    letters = [pltpu.SemaphoreType.DMA((SLOTS,))] * 4
    best = pl.pallas_call(
        kernel,
        out_shape=jax.ShapeDtypeStruct((2, HALF), jnp.float32),
        in_specs=[pl.BlockSpec(memory_space=pltpu.HBM)] * 3,
        out_specs=pl.BlockSpec(memory_space=pltpu.VMEM),
        scratch_shapes=[
            pltpu.VMEM((SLOTS, rows, depth), jnp.bfloat16),
            pltpu.VMEM((depth, TURNED), jnp.bfloat16),
            pltpu.VMEM((depth, rows), jnp.bfloat16),
            pltpu.VMEM((2, HALF), jnp.int32),
            pltpu.SMEM(member_count.shape, jnp.int32),
            pltpu.VMEM((2 * SLOTS, 8, HALF), jnp.int32),
            pltpu.VMEM((SLOTS, rows, HALF), jnp.int32),
            pltpu.VMEM((SLOTS, rows, HALF), jnp.float32),
            pltpu.VMEM((2 * SLOTS, 8, HALF), jnp.float32),
            pltpu.VMEM((2 * SLOTS, 8, HALF), jnp.float32),
            pltpu.SemaphoreType.DMA((CHUNKS,)),
            pltpu.SemaphoreType.DMA((2,)),
            *copies,
            *letters,
        ],
        compiler_params=pltpu.CompilerParams(collective_id=0, has_side_effects=True, vmem_limit_bytes=60 * 2**20),
        name="nearest_earlier",
    )(embeddings, member_order.reshape(2, HALF), member_count)
    return best.reshape(rows)


def solution(mesh):
    in_specs = (P(("grp", "row"), None), P(("grp", "row")), P())
    out_specs = P(("grp", "row"))
    return jax.shard_map(shards, mesh=mesh, in_specs=in_specs, out_specs=out_specs, check_vma=False)
```

```python
import jax
import jax.numpy as jnp
from jax import lax
from jax.experimental import pallas as pl
from jax.experimental.pallas import tpu as pltpu
from jax.sharding import PartitionSpec as P

MESH = pl.DeviceIdType.MESH
SIDE = 4
ROWS = 256
HALF = ROWS // 2
CHUNK = 64
CHUNKS = ROWS // CHUNK
ORDER = (2, 3, 0, 1)
EMPTY = 1 << 20
OTHER, NEAR, OTHER_LAST, FAR, RELAY = 4, 7, 8, 9, 10
SLOTS = 11
OTHERS = (OTHER, OTHER + 1, OTHER + 2, OTHER_LAST)
TURNED = 4 * ROWS


def kernel(
    rows_hbm, order_hbm, count_hbm, out_ref, blocks, turned, turned_own, order, count, rank_lane, rank_row, best_row,
    best_lane, mail, load_sem, word_sem, recv_sem, send_sem, branch_sem, rank_send, rank_recv, mail_send, mail_recv,
):
    group, place = lax.axis_index("grp"), lax.axis_index("row")
    core = lax.rem(group, 2)
    x, y = place // SIDE, lax.rem(place, SIDE)

    def device(main, side, flip=False):
        dx = main * (1 - core) + side * core
        dy = main * core + side * (1 - core)
        there = lax.rem(x + dx + SIDE, SIDE) * SIDE + lax.rem(y + dy + SIDE, SIDE)
        return (group + 1 - 2 * core if flip else group, there)

    partner = device(0, 0, True)
    parity = lax.rem(group // 2, 2)
    step = 1 - 2 * lax.rem(parity + core, 2)
    plane = lax.rem(group // 2 + step + SIDE, SIDE) * 2 + core
    across, ahead, behind = (plane, place), (plane, device(0, 1)[1]), (plane, device(0, -1)[1])
    along = x * core + y * (1 - core)
    near_goes_on = lax.rem(along + 3, SIDE) // 2 == parity
    far_here = lax.rem(along + 2, SIDE) // 2 == parity

    def load(c):
        at = pl.ds(c * CHUNK, CHUNK)
        return pltpu.make_async_copy(rows_hbm.at[at], blocks.at[0, at], load_sem.at[c])

    for c in ORDER:
        load(c).start()
    words = [
        pltpu.make_async_copy(order_hbm, order, word_sem.at[0]),
        pltpu.make_async_copy(count_hbm, count, word_sem.at[1]),
    ]
    for copy in words:
        copy.start()

    greeted = [device(i, 0) for i in (1, 2, 3)] + [device(0, i) for i in (1, 2, 3)]
    greeted += [partner, across, ahead, behind] + [device(i, 0, True) for i in (1, 2, 3)] + [device(0, i, True) for i in (1, 2, 3)]
    barrier = pltpu.get_barrier_semaphore()
    for there in greeted:
        pl.semaphore_signal(barrier, inc=1, device_id=there, device_id_type=MESH)

    def normalise(c):
        load(c).wait()

        @pl.loop(0, CHUNK // 16)
        def _(i):
            at = pl.ds(pl.multiple_of(c * CHUNK + i * 16, 16), 16)
            values = blocks[0, at, :].astype(jnp.float32)
            squares = jnp.sum(values * values, axis=1, keepdims=True)
            blocks[0, at, :] = (values * lax.rsqrt(squares + 1e-06)).astype(jnp.bfloat16)

    def arrival(slot, c):
        late = int(c < CHUNKS // 2)
        if slot < OTHER:
            index = (slot - 1) * CHUNKS + c
        elif slot == NEAR:
            index = 12 + c
        elif slot == RELAY:
            index = 16 + c - CHUNKS // 2
        else:
            index = {OTHER: 18, OTHER + 1: 19, OTHER + 2: 20 + late, OTHER_LAST: 22 + late, FAR: 24}[slot]
        return recv_sem.at[index]

    def move(source, slot, c, there, leaves=send_sem, chunks=1):
        at = pl.ds(c * CHUNK, chunks * CHUNK)
        return pltpu.make_async_remote_copy(
            blocks.at[source, at], blocks.at[slot, at], leaves, arrival(slot, c), device_id=there, device_id_type=MESH
        )

    sent = []

    def send(source, slot, c, there):
        move(source, slot, c, there).start()
        sent.append(slot)

    def direct(c):
        return move(NEAR, FAR, c, side_up, branch_sem)

    def out(c):
        return move(NEAR, RELAY, c, across, branch_sem)

    def relayed(c):
        return move(RELAY, FAR, c, ahead, branch_sem)

    def await_chunk(slot, c, chunks=1):
        move(slot, slot, c, partner, chunks=chunks).wait_recv()

    down, up, side_up = device(-1, 0), device(1, 0), device(0, 1)

    rank_to = [(i, device(-i, 0)) for i in (1, 2, 3)] + [(NEAR, side_up), (FAR, device(0, 2))]
    rank_to += [(OTHERS[i], device(-i, 0, True)) for i in range(4)]

    def pair(slot):
        return pl.ds(2 * slot, 2)

    def rank_copy(slot, there):
        return pltpu.make_async_remote_copy(
            rank_lane.at[pair(0)], rank_lane.at[pair(slot)], rank_send, rank_recv,
            device_id=there, device_id_type=MESH,
        )

    normalise(ORDER[0])
    for copy in words:
        copy.wait()
    slots = (core * SIDE * SIDE + place) * ROWS
    slots += lax.broadcasted_iota(jnp.int32, (2, HALF), 0) * HALF + lax.broadcasted_iota(jnp.int32, (2, HALF), 1)
    live = slots < count[group // 2]
    rank = jnp.where(live, order[...], EMPTY)
    rank_lane[pair(0)] = jnp.broadcast_to(rank[:, None, :], (2, 8, HALF))
    pl.semaphore_wait(barrier, len(greeted))
    for k, c in enumerate(ORDER):
        if k:
            normalise(c)
        send(0, 1, c, down)
        send(0, NEAR, c, side_up)
        send(0, OTHER, c, partner)
        if k == 0:
            for slot, there in rank_to:
                rank_copy(slot, there).start()

    best_row[...] = jnp.full_like(best_row, -1.0)
    best_lane[...] = jnp.full_like(best_lane, -1.0)

    def column(slot):
        for h in range(2):
            wide = jnp.broadcast_to(rank_lane[2 * slot + h][:1], (HALF, HALF))
            rank_row[slot, pl.ds(h * HALF, HALF), :] = wide.T

    def turn(slot, into, first, start=0, rows=ROWS):
        @pl.loop(0, blocks.shape[2] // 256)
        def _(i):
            at = pl.ds(pl.multiple_of(i * 256, 256), 256)
            into[at, pl.ds(first, rows)] = blocks[slot, pl.ds(start, rows), at].T

    def reduce(scores, a, start, halves, both=True):
        rows = scores.shape[0]
        mine = rank_row[a, pl.ds(start, rows), :].reshape(rows // 8, 8, HALF)
        best = best_row[a, pl.ds(start, rows), :].reshape(rows // 8, 8, HALF)
        for i, half in enumerate(halves):
            part = scores[:, i * HALF : (i + 1) * HALF].reshape(rows // 8, 8, HALF)
            earlier = rank_lane[half][None] < mine
            best = jnp.maximum(best, jnp.where(earlier, part, -1.0))
            if both:
                best_lane[half] = jnp.maximum(best_lane[half], jnp.max(jnp.where(earlier, -1.0, part), axis=0))
        best_row[a, pl.ds(start, rows), :] = best.reshape(rows, HALF)

    def meet(a, b, start=0, rows=ROWS, other=0, other_rows=ROWS, both=True):
        left, right = blocks[a, pl.ds(start, rows), :], blocks[b, pl.ds(other, other_rows), :]
        scores = lax.dot_general(left, right, (((1,), (1,)), ((), ())), preferred_element_type=jnp.float32)
        first = 2 * b + other // HALF
        reduce(scores, a, start, [first + i for i in range(other_rows // HALF)], both)

    def meet_turned(a, start, rows, columns, first, count, half):
        scores = jnp.dot(
            blocks[a, pl.ds(start, rows), :], columns[:, pl.ds(first, count)], preferred_element_type=jnp.float32
        )
        reduce(scores, a, start, [half + i for i in range(count // HALF)])

    def meet_others(a, first, last):
        @pl.loop(first, last)
        def _(i):
            meet_turned(a, 0, ROWS, turned, pl.multiple_of(i * ROWS, ROWS), ROWS, 2 * OTHER + 2 * i)

    def fold(slot, halves=(0, 1)):
        for h in halves:
            flat = best_row[slot, pl.ds(h * HALF, HALF), :].T
            found = jnp.max(flat.reshape(HALF // 8, 8, HALF), axis=0)
            best_lane[2 * slot + h] = jnp.maximum(best_lane[2 * slot + h], found)

    def await_main(k):
        slot, c = 1 + k // CHUNKS, ORDER[k % CHUNKS]
        await_chunk(slot, c)
        if k <= CHUNKS:
            send(slot, slot + 1, c, down)
        send(slot, OTHERS[slot], c, partner)
        if k == 4:
            for c in ORDER[2:] + ORDER[1:2]:
                send(0, 3, c, up)

    def await_near(c):
        await_chunk(NEAR, c)

        @pl.when(near_goes_on)
        def _():
            (direct if c in ORDER[2:] else out)(c).start()

    def await_relay(c):
        @pl.when(jnp.logical_not(near_goes_on))
        def _():
            await_chunk(RELAY, c)
            relayed(c).start()

    def await_up(k):
        await_chunk(3, k)
        send(3, OTHER_LAST, k, partner)

    column(0)
    meet(0, 0, both=False)
    turn(0, turned_own, 0)
    await_main(0)
    await_near(ORDER[0])
    letters = pl.ds(2, 2 * len(rank_to))
    ranks = pltpu.make_async_remote_copy(
        rank_lane.at[letters], rank_lane.at[letters], rank_send, rank_recv, device_id=partner, device_id_type=MESH
    )
    ranks.wait_recv()
    for slot in (1, 2, 3):
        column(slot)
    await_chunk(OTHER, 0, CHUNKS)
    turn(OTHER, turned, 0)
    meet_others(0, 0, 1)
    await_main(1)
    await_near(ORDER[1])
    await_relay(ORDER[0])
    await_main(2)
    await_near(ORDER[2])
    await_relay(ORDER[1])
    await_main(3)
    await_near(ORDER[3])
    meet_turned(1, 0, ROWS, turned_own, 0, ROWS, 0)
    meet_others(1, 0, 1)
    await_main(4)
    await_chunk(OTHER + 1, 0, CHUNKS)
    turn(OTHER + 1, turned, ROWS)
    meet_others(1, 1, 2)
    turn(NEAR, turned, 3 * ROWS)
    await_main(5)
    meet_others(0, 3, 4)
    meet_others(1, 3, 4)
    meet_turned(2, HALF, HALF, turned_own, 0, ROWS, 0)
    meet_turned(2, HALF, HALF, turned, 0, 2 * ROWS, 2 * OTHER)
    meet_turned(2, HALF, HALF, turned, 3 * ROWS, ROWS, 2 * NEAR)
    await_main(6)
    await_up(ORDER[2])
    await_chunk(OTHER + 2, CHUNKS // 2, CHUNKS // 2)
    turn(OTHER + 2, turned, 2 * ROWS + HALF, HALF, HALF)

    @pl.when(far_here)
    def _():
        await_chunk(FAR, 0, CHUNKS)

        @pl.loop(0, 2)
        def _(a):
            meet(a, FAR)

    await_main(7)
    meet_turned(2, 0, HALF, turned_own, 0, HALF, 0)
    meet_turned(2, 0, HALF, turned, 0, 2 * ROWS, 2 * OTHER)
    meet_turned(2, 0, HALF, turned, 3 * ROWS, ROWS, 2 * NEAR)
    await_chunk(OTHER + 2, 0, CHUNKS // 2)
    turn(OTHER + 2, turned, 2 * ROWS, 0, HALF)
    meet_others(2, 2, 3)
    await_up(ORDER[3])

    @pl.when(far_here)
    def _():
        meet(2, FAR)

    meet_turned(3, 0, HALF, turned, 0, TURNED, 2 * OTHER)
    for slot in (0, 1, 2):
        fold(slot)

    owners = [(i, device(i, 0)) for i in (1, 2, 3)] + [(NEAR, device(0, -1)), (FAR, device(0, -2))]
    owners += [(OTHERS[i], device(0, i, True)) for i in range(4)]

    def mail_copy(slot, there):
        return pltpu.make_async_remote_copy(
            best_lane.at[pair(slot)], mail.at[pair(slot)], mail_send, mail_recv,
            device_id=there, device_id_type=MESH,
        )

    def post(*slots):
        for slot, there in owners:
            if slot in slots:
                mail_copy(slot, there).start()

    post(1, 2)
    await_main(8)
    await_up(ORDER[1])
    meet_turned(3, HALF, HALF, turned, 0, TURNED, 2 * OTHER)
    post(OTHER, OTHER + 1, OTHER + 2, NEAR)

    @pl.when(far_here)
    def _():
        meet(3, FAR)

    post(FAR)
    await_chunk(OTHER_LAST, 0, CHUNKS // 2)
    meet(3, OTHER_LAST, other_rows=HALF)
    fold(3, (0,))
    await_chunk(OTHER_LAST, CHUNKS // 2, CHUNKS // 2)
    meet(3, OTHER_LAST, HALF, HALF, HALF, HALF)
    post(OTHER_LAST)
    fold(3, (1,))
    post(3)

    whole = pl.ds(0, len(sent) // CHUNKS)
    pltpu.make_async_copy(blocks.at[whole], blocks.at[whole], send_sem).wait()

    @pl.when(near_goes_on)
    def _():
        pltpu.make_async_copy(blocks.at[0], blocks.at[0], branch_sem).wait()

    @pl.when(jnp.logical_not(near_goes_on))
    def _():
        half = blocks.at[0, pl.ds(0, HALF)]
        pltpu.make_async_copy(half, half, branch_sem).wait()

    ranks.wait_send()
    mails = pltpu.make_async_remote_copy(
        best_lane.at[letters], mail.at[letters], mail_send, mail_recv, device_id=partner, device_id_type=MESH
    )
    mails.wait_recv()
    found = best_lane[pair(0)]
    for slot, there in owners:
        found = jnp.maximum(found, mail[pair(slot)])
    out_ref[...] = jnp.where(rank_lane[pair(0)][:, 0, :] < EMPTY, jnp.max(found, axis=1), -1.0)
    mails.wait_send()


def shards(embeddings, member_order, member_count):
    rows, depth = embeddings.shape
    best = pl.pallas_call(
        kernel,
        out_shape=jax.ShapeDtypeStruct((2, HALF), jnp.float32),
        in_specs=[pl.BlockSpec(memory_space=pltpu.HBM)] * 3,
        out_specs=pl.BlockSpec(memory_space=pltpu.VMEM),
        scratch_shapes=[
            pltpu.VMEM((SLOTS, rows, depth), jnp.bfloat16),
            pltpu.VMEM((depth, TURNED), jnp.bfloat16),
            pltpu.VMEM((depth, rows), jnp.bfloat16),
            pltpu.VMEM((2, HALF), jnp.int32),
            pltpu.SMEM(member_count.shape, jnp.int32),
            pltpu.VMEM((2 * SLOTS, 8, HALF), jnp.int32),
            pltpu.VMEM((SLOTS, rows, HALF), jnp.int32),
            pltpu.VMEM((SLOTS, rows, HALF), jnp.float32),
            pltpu.VMEM((2 * SLOTS, 8, HALF), jnp.float32),
            pltpu.VMEM((2 * SLOTS, 8, HALF), jnp.float32),
            pltpu.SemaphoreType.DMA((CHUNKS,)),
            pltpu.SemaphoreType.DMA((2,)),
            pltpu.SemaphoreType.DMA((25,)),
            *[pltpu.SemaphoreType.DMA] * 6,
        ],
        compiler_params=pltpu.CompilerParams(collective_id=0, has_side_effects=True, vmem_limit_bytes=60 * 2**20),
        name="nearest_earlier",
    )(embeddings, member_order.reshape(2, HALF), member_count)
    return best.reshape(rows)


def solution(mesh):
    in_specs = (P(("grp", "row"), None), P(("grp", "row")), P())
    out_specs = P(("grp", "row"))
    return jax.shard_map(shards, mesh=mesh, in_specs=in_specs, out_specs=out_specs, check_vma=False)
```

```python
import jax
import jax.numpy as jnp
from jax import lax
from jax.experimental import pallas as pl
from jax.experimental.pallas import tpu as pltpu
from jax.sharding import PartitionSpec as P

MESH = pl.DeviceIdType.MESH
SIDE = 4
ROWS = 256
HALF = ROWS // 2
CHUNK = 64
CHUNKS = ROWS // CHUNK
ORDER = (2, 3, 0, 1)
EMPTY = 1 << 20
OTHER, NEAR, FAR, OTHER_LAST, RELAY = 4, 7, 8, 9, 10
SLOTS = 11
OTHERS = (OTHER, OTHER + 1, OTHER + 2, OTHER_LAST)
TURNED = 5 * ROWS


def kernel(
    rows_hbm, order_hbm, count_hbm, out_ref, blocks, turned, turned_own, order, count, rank_lane, rank_row, best_row,
    best_lane, mail, load_sem, word_sem, recv_sem, send_sem, branch_sem, rank_send, rank_recv, mail_send, mail_recv,
):
    group, place = lax.axis_index("grp"), lax.axis_index("row")
    core = lax.rem(group, 2)
    x, y = place // SIDE, lax.rem(place, SIDE)

    def device(main, side, flip=False):
        dx = main * (1 - core) + side * core
        dy = main * core + side * (1 - core)
        there = lax.rem(x + dx + SIDE, SIDE) * SIDE + lax.rem(y + dy + SIDE, SIDE)
        return (group + 1 - 2 * core if flip else group, there)

    partner = device(0, 0, True)
    parity = lax.rem(group // 2, 2)
    step = 1 - 2 * lax.rem(parity + core, 2)
    plane = lax.rem(group // 2 + step + SIDE, SIDE) * 2 + core
    across, ahead, behind = (plane, place), (plane, device(0, 1)[1]), (plane, device(0, -1)[1])
    along = x * core + y * (1 - core)
    near_goes_on = lax.rem(along + 3, SIDE) // 2 == parity
    far_here = lax.rem(along + 2, SIDE) // 2 == parity

    def load(c):
        at = pl.ds(c * CHUNK, CHUNK)
        return pltpu.make_async_copy(rows_hbm.at[at], blocks.at[0, at], load_sem.at[c])

    for c in ORDER:
        load(c).start()
    words = [
        pltpu.make_async_copy(order_hbm, order, word_sem.at[0]),
        pltpu.make_async_copy(count_hbm, count, word_sem.at[1]),
    ]
    for copy in words:
        copy.start()

    greeted = [device(1, 0), device(-1, 0), device(0, -1), partner, across, behind, device(2, 0), device(0, -2)]
    greeted += [device(0, i, True) for i in (1, 2, 3)]
    barrier = pltpu.get_barrier_semaphore()
    for there in greeted:
        pl.semaphore_signal(barrier, inc=1, device_id=there, device_id_type=MESH)

    def normalise(c):
        load(c).wait()

        @pl.loop(0, CHUNK // 16)
        def _(i):
            at = pl.ds(pl.multiple_of(c * CHUNK + i * 16, 16), 16)
            values = blocks[0, at, :].astype(jnp.float32)
            squares = jnp.sum(values * values, axis=1, keepdims=True)
            blocks[0, at, :] = (values * lax.rsqrt(squares + 1e-06)).astype(jnp.bfloat16)

    def arrival(slot, c):
        late = int(c < CHUNKS // 2)
        if slot < OTHER:
            index = (slot - 1) * CHUNKS + c
        elif slot == NEAR:
            index = 12 + c
        elif slot == RELAY:
            index = 16 + c - CHUNKS // 2
        else:
            index = {OTHER: 18, OTHER + 1: 19, OTHER + 2: 20 + late, OTHER_LAST: 22 + late, FAR: 24}[slot]
        return recv_sem.at[index]

    def move(source, slot, c, there, leaves=send_sem, chunks=1):
        at = pl.ds(c * CHUNK, chunks * CHUNK)
        return pltpu.make_async_remote_copy(
            blocks.at[source, at], blocks.at[slot, at], leaves, arrival(slot, c), device_id=there, device_id_type=MESH
        )

    sent = []

    def send(source, slot, c, there):
        move(source, slot, c, there).start()
        sent.append(slot)

    def direct(c):
        return move(NEAR, FAR, c, side_up, branch_sem)

    def out(c):
        return move(NEAR, RELAY, c, across, branch_sem)

    def relayed(c):
        return move(RELAY, FAR, c, ahead, branch_sem)

    def await_chunk(slot, c, chunks=1):
        move(slot, slot, c, partner, chunks=chunks).wait_recv()

    down, up, side_up = device(-1, 0), device(1, 0), device(0, 1)

    rank_to = [(i, device(-i, 0)) for i in (1, 2, 3)] + [(NEAR, side_up), (FAR, device(0, 2))]
    rank_to += [(OTHERS[i], device(-i, 0, True)) for i in range(4)]

    def pair(slot):
        return pl.ds(2 * slot, 2)

    def rank_copy(slot, there):
        return pltpu.make_async_remote_copy(
            rank_lane.at[pair(0)], rank_lane.at[pair(slot)], rank_send, rank_recv,
            device_id=there, device_id_type=MESH,
        )

    normalise(ORDER[0])
    for copy in words:
        copy.wait()
    slots = (core * SIDE * SIDE + place) * ROWS
    slots += lax.broadcasted_iota(jnp.int32, (2, HALF), 0) * HALF + lax.broadcasted_iota(jnp.int32, (2, HALF), 1)
    live = slots < count[group // 2]
    rank = jnp.where(live, order[...], EMPTY)
    rank_lane[pair(0)] = jnp.broadcast_to(rank[:, None, :], (2, 8, HALF))
    pl.semaphore_wait(barrier, len(greeted))
    for k, c in enumerate(ORDER):
        if k:
            normalise(c)
        send(0, 1, c, down)
        send(0, NEAR, c, side_up)
        send(0, OTHER, c, partner)
        if k == 0:
            for slot, there in rank_to:
                rank_copy(slot, there).start()

    best_row[...] = jnp.full_like(best_row, -1.0)
    best_lane[...] = jnp.full_like(best_lane, -1.0)

    def column(slot):
        for h in range(2):
            wide = jnp.broadcast_to(rank_lane[2 * slot + h][:1], (HALF, HALF))
            rank_row[slot, pl.ds(h * HALF, HALF), :] = wide.T

    def turn(slot, into, first, start=0, rows=ROWS):
        @pl.loop(0, blocks.shape[2] // 256)
        def _(i):
            at = pl.ds(pl.multiple_of(i * 256, 256), 256)
            into[at, pl.ds(first, rows)] = blocks[slot, pl.ds(start, rows), at].T

    def reduce(scores, a, start, halves, both=True):
        rows = scores.shape[0]
        mine = rank_row[a, pl.ds(start, rows), :].reshape(rows // 8, 8, HALF)
        best = best_row[a, pl.ds(start, rows), :].reshape(rows // 8, 8, HALF)
        for i, half in enumerate(halves):
            part = scores[:, i * HALF : (i + 1) * HALF].reshape(rows // 8, 8, HALF)
            earlier = rank_lane[half][None] < mine
            best = jnp.maximum(best, jnp.where(earlier, part, -1.0))
            if both:
                best_lane[half] = jnp.maximum(best_lane[half], jnp.max(jnp.where(earlier, -1.0, part), axis=0))
        best_row[a, pl.ds(start, rows), :] = best.reshape(rows, HALF)

    def meet(a, b, start=0, rows=ROWS, other=0, other_rows=ROWS, both=True):
        left, right = blocks[a, pl.ds(start, rows), :], blocks[b, pl.ds(other, other_rows), :]
        scores = lax.dot_general(left, right, (((1,), (1,)), ((), ())), preferred_element_type=jnp.float32)
        first = 2 * b + other // HALF
        reduce(scores, a, start, [first + i for i in range(other_rows // HALF)], both)

    def meet_turned(a, start, rows, columns, first, count, half):
        scores = jnp.dot(
            blocks[a, pl.ds(start, rows), :], columns[:, pl.ds(first, count)], preferred_element_type=jnp.float32
        )
        reduce(scores, a, start, [half + i for i in range(count // HALF)])

    def meet_others(a, first, last):
        @pl.loop(first, last)
        def _(i):
            meet_turned(a, 0, ROWS, turned, pl.multiple_of(i * ROWS, ROWS), ROWS, 2 * OTHER + 2 * i)

    def fold(slot, halves=(0, 1)):
        for h in halves:
            flat = best_row[slot, pl.ds(h * HALF, HALF), :].T
            found = jnp.max(flat.reshape(HALF // 8, 8, HALF), axis=0)
            best_lane[2 * slot + h] = jnp.maximum(best_lane[2 * slot + h], found)

    def await_main(k):
        slot, c = 1 + k // CHUNKS, ORDER[k % CHUNKS]
        await_chunk(slot, c)
        if k <= CHUNKS:
            send(slot, slot + 1, c, down)
        send(slot, OTHERS[slot], c, partner)
        if k == 4:
            for c in ORDER[2:] + ORDER[1:2]:
                send(0, 3, c, up)

    def await_near(c):
        await_chunk(NEAR, c)

        @pl.when(near_goes_on)
        def _():
            (direct if c in ORDER[2:] else out)(c).start()

    def await_relay(c):
        @pl.when(jnp.logical_not(near_goes_on))
        def _():
            await_chunk(RELAY, c)
            relayed(c).start()

    def await_up(k):
        await_chunk(3, k)
        send(3, OTHER_LAST, k, partner)

    column(0)
    meet(0, 0, both=False)
    turn(0, turned_own, 0)
    await_main(0)
    await_near(ORDER[0])
    letters = pl.ds(2, 2 * len(rank_to))
    ranks = pltpu.make_async_remote_copy(
        rank_lane.at[letters], rank_lane.at[letters], rank_send, rank_recv, device_id=partner, device_id_type=MESH
    )
    ranks.wait_recv()
    for slot in (1, 2, 3):
        column(slot)
    await_chunk(OTHER, 0, CHUNKS)
    turn(OTHER, turned, 0)
    meet_others(0, 0, 1)
    await_main(1)
    await_near(ORDER[1])
    await_relay(ORDER[0])
    await_main(2)
    await_near(ORDER[2])
    await_relay(ORDER[1])
    await_main(3)
    await_near(ORDER[3])
    meet_turned(1, 0, ROWS, turned_own, 0, ROWS, 0)
    meet_others(1, 0, 1)
    await_main(4)
    await_chunk(OTHER + 1, 0, CHUNKS)
    turn(OTHER + 1, turned, ROWS)
    meet_others(1, 1, 2)
    turn(NEAR, turned, 3 * ROWS)
    await_main(5)
    meet_others(0, 3, 4)
    meet_others(1, 3, 4)
    meet_turned(2, HALF, HALF, turned_own, 0, ROWS, 0)
    meet_turned(2, HALF, HALF, turned, 0, 2 * ROWS, 2 * OTHER)
    meet_turned(2, HALF, HALF, turned, 3 * ROWS, ROWS, 2 * NEAR)
    await_main(6)
    await_up(ORDER[2])
    await_chunk(OTHER + 2, CHUNKS // 2, CHUNKS // 2)
    turn(OTHER + 2, turned, 2 * ROWS + HALF, HALF, HALF)

    @pl.when(far_here)
    def _():
        await_chunk(FAR, 0, CHUNKS)
        turn(FAR, turned, 4 * ROWS)

        @pl.loop(0, 2)
        def _(a):
            meet_turned(a, 0, ROWS, turned, 4 * ROWS, ROWS, 2 * FAR)

    await_main(7)
    meet_turned(2, 0, HALF, turned_own, 0, HALF, 0)
    meet_turned(2, 0, HALF, turned, 0, 2 * ROWS, 2 * OTHER)
    meet_turned(2, 0, HALF, turned, 3 * ROWS, ROWS, 2 * NEAR)
    await_chunk(OTHER + 2, 0, CHUNKS // 2)
    turn(OTHER + 2, turned, 2 * ROWS, 0, HALF)
    meet_others(2, 2, 3)
    await_up(ORDER[3])

    @pl.when(far_here)
    def _():
        meet_turned(2, 0, ROWS, turned, 4 * ROWS, ROWS, 2 * FAR)
        meet_turned(3, 0, HALF, turned, 4 * ROWS, ROWS, 2 * FAR)

    meet_turned(3, 0, HALF, turned, 0, 4 * ROWS, 2 * OTHER)
    for slot in (0, 1, 2):
        fold(slot)

    owners = [(i, device(i, 0)) for i in (1, 2, 3)] + [(NEAR, device(0, -1)), (FAR, device(0, -2))]
    owners += [(OTHERS[i], device(0, i, True)) for i in range(4)]

    def mail_copy(slot, there):
        return pltpu.make_async_remote_copy(
            best_lane.at[pair(slot)], mail.at[pair(slot)], mail_send, mail_recv,
            device_id=there, device_id_type=MESH,
        )

    def post(*slots):
        for slot, there in owners:
            if slot in slots:
                mail_copy(slot, there).start()

    post(1, 2)
    await_main(8)
    await_up(ORDER[1])

    @pl.when(far_here)
    def _():
        meet_turned(3, HALF, HALF, turned, 0, TURNED, 2 * OTHER)

    @pl.when(jnp.logical_not(far_here))
    def _():
        meet_turned(3, HALF, HALF, turned, 0, 4 * ROWS, 2 * OTHER)

    post(OTHER, OTHER + 1, OTHER + 2, NEAR, FAR)
    await_chunk(OTHER_LAST, 0, CHUNKS // 2)
    meet(3, OTHER_LAST, other_rows=HALF)
    fold(3, (0,))
    await_chunk(OTHER_LAST, CHUNKS // 2, CHUNKS // 2)
    meet(3, OTHER_LAST, HALF, HALF, HALF, HALF)
    post(OTHER_LAST)
    fold(3, (1,))
    post(3)

    whole = pl.ds(0, len(sent) // CHUNKS)
    pltpu.make_async_copy(blocks.at[whole], blocks.at[whole], send_sem).wait()

    @pl.when(near_goes_on)
    def _():
        pltpu.make_async_copy(blocks.at[0], blocks.at[0], branch_sem).wait()

    @pl.when(jnp.logical_not(near_goes_on))
    def _():
        half = blocks.at[0, pl.ds(0, HALF)]
        pltpu.make_async_copy(half, half, branch_sem).wait()

    ranks.wait_send()
    mails = pltpu.make_async_remote_copy(
        best_lane.at[letters], mail.at[letters], mail_send, mail_recv, device_id=partner, device_id_type=MESH
    )
    mails.wait_recv()
    found = best_lane[pair(0)]
    for slot, there in owners:
        found = jnp.maximum(found, mail[pair(slot)])
    out_ref[...] = jnp.where(rank_lane[pair(0)][:, 0, :] < EMPTY, jnp.max(found, axis=1), -1.0)
    mails.wait_send()


def shards(embeddings, member_order, member_count):
    rows, depth = embeddings.shape
    best = pl.pallas_call(
        kernel,
        out_shape=jax.ShapeDtypeStruct((2, HALF), jnp.float32),
        in_specs=[pl.BlockSpec(memory_space=pltpu.HBM)] * 3,
        out_specs=pl.BlockSpec(memory_space=pltpu.VMEM),
        scratch_shapes=[
            pltpu.VMEM((SLOTS, rows, depth), jnp.bfloat16),
            pltpu.VMEM((depth, TURNED), jnp.bfloat16),
            pltpu.VMEM((depth, rows), jnp.bfloat16),
            pltpu.VMEM((2, HALF), jnp.int32),
            pltpu.SMEM(member_count.shape, jnp.int32),
            pltpu.VMEM((2 * SLOTS, 8, HALF), jnp.int32),
            pltpu.VMEM((SLOTS, rows, HALF), jnp.int32),
            pltpu.VMEM((SLOTS, rows, HALF), jnp.float32),
            pltpu.VMEM((2 * SLOTS, 8, HALF), jnp.float32),
            pltpu.VMEM((2 * SLOTS, 8, HALF), jnp.float32),
            pltpu.SemaphoreType.DMA((CHUNKS,)),
            pltpu.SemaphoreType.DMA((2,)),
            pltpu.SemaphoreType.DMA((25,)),
            *[pltpu.SemaphoreType.DMA] * 6,
        ],
        compiler_params=pltpu.CompilerParams(collective_id=0, has_side_effects=True, vmem_limit_bytes=60 * 2**20),
        name="nearest_earlier",
    )(embeddings, member_order.reshape(2, HALF), member_count)
    return best.reshape(rows)


def solution(mesh):
    in_specs = (P(("grp", "row"), None), P(("grp", "row")), P())
    out_specs = P(("grp", "row"))
    return jax.shard_map(shards, mesh=mesh, in_specs=in_specs, out_specs=out_specs, check_vma=False)
```

```python
import jax
import jax.numpy as jnp
from jax import lax
from jax.experimental import pallas as pl
from jax.experimental.pallas import tpu as pltpu
from jax.sharding import PartitionSpec as P

MESH = pl.DeviceIdType.MESH
SIDE = 4
ROWS = 256
HALF = ROWS // 2
CHUNK = 64
CHUNKS = ROWS // CHUNK
ORDER = (2, 3, 0, 1)
EMPTY = 1 << 20
OTHER, NEAR, FAR, OTHER_LAST, RELAY = 4, 7, 8, 9, 10
SLOTS = 11
OTHERS = (OTHER, OTHER + 1, OTHER + 2, OTHER_LAST)
TURNED = 5 * ROWS


def kernel(
    rows_hbm, order_hbm, count_hbm, out_ref, blocks, turned, turned_own, order, count, rank_lane, rank_row, best_row,
    best_lane, mail, load_sem, word_sem, recv_sem, send_sem, branch_sem, rank_send, rank_recv, mail_send, mail_recv,
):
    group, place = lax.axis_index("grp"), lax.axis_index("row")
    core = lax.rem(group, 2)
    x, y = place // SIDE, lax.rem(place, SIDE)

    def device(main, side, flip=False):
        dx = main * (1 - core) + side * core
        dy = main * core + side * (1 - core)
        there = lax.rem(x + dx + SIDE, SIDE) * SIDE + lax.rem(y + dy + SIDE, SIDE)
        return (group + 1 - 2 * core if flip else group, there)

    partner = device(0, 0, True)
    parity = lax.rem(group // 2, 2)
    step = 1 - 2 * lax.rem(parity + core, 2)
    plane = lax.rem(group // 2 + step + SIDE, SIDE) * 2 + core
    across, ahead, behind = (plane, place), (plane, device(0, 1)[1]), (plane, device(0, -1)[1])
    along = x * core + y * (1 - core)
    near_goes_on = lax.rem(along + 3, SIDE) // 2 == parity
    far_here = lax.rem(along + 2, SIDE) // 2 == parity

    def load(c):
        at = pl.ds(c * CHUNK, CHUNK)
        return pltpu.make_async_copy(rows_hbm.at[at], blocks.at[0, at], load_sem.at[c])

    for c in ORDER:
        load(c).start()
    words = [
        pltpu.make_async_copy(order_hbm, order, word_sem.at[0]),
        pltpu.make_async_copy(count_hbm, count, word_sem.at[1]),
    ]
    for copy in words:
        copy.start()

    greeted = [device(1, 0), device(-1, 0), device(0, -1), partner, across, behind, device(2, 0), device(0, -2)]
    greeted += [device(0, i, True) for i in (1, 2, 3)]
    barrier = pltpu.get_barrier_semaphore()
    for there in greeted:
        pl.semaphore_signal(barrier, inc=1, device_id=there, device_id_type=MESH)

    def normalise(c):
        load(c).wait()

        @pl.loop(0, CHUNK // 16)
        def _(i):
            at = pl.ds(pl.multiple_of(c * CHUNK + i * 16, 16), 16)
            values = blocks[0, at, :].astype(jnp.float32)
            squares = jnp.sum(values * values, axis=1, keepdims=True)
            blocks[0, at, :] = (values * lax.rsqrt(squares + 1e-06)).astype(jnp.bfloat16)

    def arrival(slot, c):
        late = int(c < CHUNKS // 2)
        if slot < OTHER:
            index = (slot - 1) * CHUNKS + c
        elif slot == NEAR:
            index = 12 + c
        elif slot == RELAY:
            index = 16 + c - CHUNKS // 2
        else:
            index = {OTHER: 18, OTHER + 1: 19, OTHER + 2: 20 + late, OTHER_LAST: 22 + late, FAR: 24}[slot]
        return recv_sem.at[index]

    def move(source, slot, c, there, leaves=send_sem, chunks=1):
        at = pl.ds(c * CHUNK, chunks * CHUNK)
        return pltpu.make_async_remote_copy(
            blocks.at[source, at], blocks.at[slot, at], leaves, arrival(slot, c), device_id=there, device_id_type=MESH
        )

    sent = []

    def send(source, slot, c, there):
        move(source, slot, c, there).start()
        sent.append(slot)

    def direct(c):
        return move(NEAR, FAR, c, side_up, branch_sem)

    def out(c):
        return move(NEAR, RELAY, c, across, branch_sem)

    def relayed(c):
        return move(RELAY, FAR, c, ahead, branch_sem)

    def await_chunk(slot, c, chunks=1):
        move(slot, slot, c, partner, chunks=chunks).wait_recv()

    down, up, side_up = device(-1, 0), device(1, 0), device(0, 1)

    rank_to = [(i, device(-i, 0)) for i in (1, 2, 3)] + [(NEAR, side_up), (FAR, device(0, 2))]
    rank_to += [(OTHERS[i], device(-i, 0, True)) for i in range(4)]

    def pair(slot):
        return pl.ds(2 * slot, 2)

    def rank_copy(slot, there):
        return pltpu.make_async_remote_copy(
            rank_lane.at[pair(0)], rank_lane.at[pair(slot)], rank_send, rank_recv,
            device_id=there, device_id_type=MESH,
        )

    normalise(ORDER[0])
    for copy in words:
        copy.wait()
    slots = (core * SIDE * SIDE + place) * ROWS
    slots += lax.broadcasted_iota(jnp.int32, (2, HALF), 0) * HALF + lax.broadcasted_iota(jnp.int32, (2, HALF), 1)
    live = slots < count[group // 2]
    rank = jnp.where(live, order[...], EMPTY)
    rank_lane[pair(0)] = jnp.broadcast_to(rank[:, None, :], (2, 8, HALF))
    pl.semaphore_wait(barrier, len(greeted))
    for slot, there in rank_to:
        rank_copy(slot, there).start()
    for k, c in enumerate(ORDER):
        if k:
            normalise(c)
        send(0, 1, c, down)
        send(0, NEAR, c, side_up)
        send(0, OTHER, c, partner)

    best_row[...] = jnp.full_like(best_row, -1.0)
    best_lane[...] = jnp.full_like(best_lane, -1.0)

    def column(slot):
        for h in range(2):
            wide = jnp.broadcast_to(rank_lane[2 * slot + h][:1], (HALF, HALF))
            rank_row[slot, pl.ds(h * HALF, HALF), :] = wide.T

    def turn(slot, into, first, start=0, rows=ROWS):
        @pl.loop(0, blocks.shape[2] // 256)
        def _(i):
            at = pl.ds(pl.multiple_of(i * 256, 256), 256)
            into[at, pl.ds(first, rows)] = blocks[slot, pl.ds(start, rows), at].T

    def reduce(scores, a, start, halves, both=True):
        rows = scores.shape[0]
        mine = rank_row[a, pl.ds(start, rows), :].reshape(rows // 8, 8, HALF)
        best = best_row[a, pl.ds(start, rows), :].reshape(rows // 8, 8, HALF)
        for i, half in enumerate(halves):
            part = scores[:, i * HALF : (i + 1) * HALF].reshape(rows // 8, 8, HALF)
            earlier = rank_lane[half][None] < mine
            best = jnp.maximum(best, jnp.where(earlier, part, -1.0))
            if both:
                best_lane[half] = jnp.maximum(best_lane[half], jnp.max(jnp.where(earlier, -1.0, part), axis=0))
        best_row[a, pl.ds(start, rows), :] = best.reshape(rows, HALF)

    def meet(a, b, start=0, rows=ROWS, other=0, other_rows=ROWS, both=True):
        left, right = blocks[a, pl.ds(start, rows), :], blocks[b, pl.ds(other, other_rows), :]
        scores = lax.dot_general(left, right, (((1,), (1,)), ((), ())), preferred_element_type=jnp.float32)
        first = 2 * b + other // HALF
        reduce(scores, a, start, [first + i for i in range(other_rows // HALF)], both)

    def meet_turned(a, start, rows, columns, first, count, half):
        scores = jnp.dot(
            blocks[a, pl.ds(start, rows), :], columns[:, pl.ds(first, count)], preferred_element_type=jnp.float32
        )
        reduce(scores, a, start, [half + i for i in range(count // HALF)])

    def meet_others(a, first, last):
        @pl.loop(first, last)
        def _(i):
            meet_turned(a, 0, ROWS, turned, pl.multiple_of(i * ROWS, ROWS), ROWS, 2 * OTHER + 2 * i)

    def fold(slot, halves=(0, 1)):
        for h in halves:
            flat = best_row[slot, pl.ds(h * HALF, HALF), :].T
            found = jnp.max(flat.reshape(HALF // 8, 8, HALF), axis=0)
            best_lane[2 * slot + h] = jnp.maximum(best_lane[2 * slot + h], found)

    def await_main(k):
        slot, c = 1 + k // CHUNKS, ORDER[k % CHUNKS]
        await_chunk(slot, c)
        if k <= CHUNKS:
            send(slot, slot + 1, c, down)
        send(slot, OTHERS[slot], c, partner)
        if k == 4:
            for c in ORDER[2:] + ORDER[1:2]:
                send(0, 3, c, up)

    def await_near(c):
        await_chunk(NEAR, c)

        @pl.when(near_goes_on)
        def _():
            (direct if c in ORDER[2:] else out)(c).start()

    def await_relay(c):
        @pl.when(jnp.logical_not(near_goes_on))
        def _():
            await_chunk(RELAY, c)
            relayed(c).start()

    def await_up(k):
        await_chunk(3, k)
        send(3, OTHER_LAST, k, partner)

    column(0)
    meet(0, 0, both=False)
    turn(0, turned_own, 0)
    await_main(0)
    await_near(ORDER[0])
    letters = pl.ds(2, 2 * len(rank_to))
    ranks = pltpu.make_async_remote_copy(
        rank_lane.at[letters], rank_lane.at[letters], rank_send, rank_recv, device_id=partner, device_id_type=MESH
    )
    ranks.wait_recv()
    for slot in (1, 2, 3):
        column(slot)
    await_chunk(OTHER, 0, CHUNKS)
    turn(OTHER, turned, 0)
    meet_others(0, 0, 1)
    await_main(1)
    await_near(ORDER[1])
    await_relay(ORDER[0])
    await_main(2)
    await_near(ORDER[2])
    await_relay(ORDER[1])
    await_main(3)
    await_near(ORDER[3])
    meet_turned(1, 0, ROWS, turned_own, 0, ROWS, 0)
    meet_others(1, 0, 1)
    await_main(4)
    await_chunk(OTHER + 1, 0, CHUNKS)
    turn(OTHER + 1, turned, ROWS)
    meet_others(1, 1, 2)
    turn(NEAR, turned, 3 * ROWS)
    await_main(5)
    meet_others(0, 3, 4)
    meet_others(1, 3, 4)
    meet_turned(2, HALF, HALF, turned_own, 0, ROWS, 0)
    meet_turned(2, HALF, HALF, turned, 0, 2 * ROWS, 2 * OTHER)
    meet_turned(2, HALF, HALF, turned, 3 * ROWS, ROWS, 2 * NEAR)
    await_main(6)
    await_up(ORDER[2])
    await_chunk(OTHER + 2, CHUNKS // 2, CHUNKS // 2)
    turn(OTHER + 2, turned, 2 * ROWS + HALF, HALF, HALF)

    @pl.when(far_here)
    def _():
        await_chunk(FAR, 0, CHUNKS)
        turn(FAR, turned, 4 * ROWS)

        @pl.loop(0, 2)
        def _(a):
            meet_turned(a, 0, ROWS, turned, 4 * ROWS, ROWS, 2 * FAR)

    await_main(7)
    meet_turned(2, 0, HALF, turned_own, 0, HALF, 0)
    meet_turned(2, 0, HALF, turned, 0, 2 * ROWS, 2 * OTHER)
    meet_turned(2, 0, HALF, turned, 3 * ROWS, ROWS, 2 * NEAR)
    await_chunk(OTHER + 2, 0, CHUNKS // 2)
    turn(OTHER + 2, turned, 2 * ROWS, 0, HALF)
    meet_others(2, 2, 3)
    await_up(ORDER[3])

    @pl.when(far_here)
    def _():
        meet_turned(2, 0, ROWS, turned, 4 * ROWS, ROWS, 2 * FAR)
        meet_turned(3, 0, HALF, turned, 4 * ROWS, ROWS, 2 * FAR)

    meet_turned(3, 0, HALF, turned, 0, 4 * ROWS, 2 * OTHER)
    for slot in (0, 1, 2):
        fold(slot)

    owners = [(i, device(i, 0)) for i in (1, 2, 3)] + [(NEAR, device(0, -1)), (FAR, device(0, -2))]
    owners += [(OTHERS[i], device(0, i, True)) for i in range(4)]

    def mail_copy(slot, there):
        return pltpu.make_async_remote_copy(
            best_lane.at[pair(slot)], mail.at[pair(slot)], mail_send, mail_recv,
            device_id=there, device_id_type=MESH,
        )

    def post(*slots):
        for slot, there in owners:
            if slot in slots:
                mail_copy(slot, there).start()

    post(1, 2)
    await_main(8)
    await_up(ORDER[1])

    @pl.when(far_here)
    def _():
        meet_turned(3, HALF, HALF, turned, 0, TURNED, 2 * OTHER)

    @pl.when(jnp.logical_not(far_here))
    def _():
        meet_turned(3, HALF, HALF, turned, 0, 4 * ROWS, 2 * OTHER)

    post(OTHER, OTHER + 1, OTHER + 2, NEAR, FAR)
    await_chunk(OTHER_LAST, 0, CHUNKS // 2)
    meet(3, OTHER_LAST, other_rows=HALF)
    fold(3, (0,))
    await_chunk(OTHER_LAST, CHUNKS // 2, CHUNKS // 2)
    meet(3, OTHER_LAST, HALF, HALF, HALF, HALF)
    post(OTHER_LAST)
    fold(3, (1,))
    post(3)

    whole = pl.ds(0, len(sent) // CHUNKS)
    pltpu.make_async_copy(blocks.at[whole], blocks.at[whole], send_sem).wait()

    @pl.when(near_goes_on)
    def _():
        pltpu.make_async_copy(blocks.at[0], blocks.at[0], branch_sem).wait()

    @pl.when(jnp.logical_not(near_goes_on))
    def _():
        half = blocks.at[0, pl.ds(0, HALF)]
        pltpu.make_async_copy(half, half, branch_sem).wait()

    ranks.wait_send()
    mails = pltpu.make_async_remote_copy(
        best_lane.at[letters], mail.at[letters], mail_send, mail_recv, device_id=partner, device_id_type=MESH
    )
    mails.wait_recv()
    found = best_lane[pair(0)]
    for slot, there in owners:
        found = jnp.maximum(found, mail[pair(slot)])
    out_ref[...] = jnp.where(rank_lane[pair(0)][:, 0, :] < EMPTY, jnp.max(found, axis=1), -1.0)
    mails.wait_send()


def shards(embeddings, member_order, member_count):
    rows, depth = embeddings.shape
    best = pl.pallas_call(
        kernel,
        out_shape=jax.ShapeDtypeStruct((2, HALF), jnp.float32),
        in_specs=[pl.BlockSpec(memory_space=pltpu.HBM)] * 3,
        out_specs=pl.BlockSpec(memory_space=pltpu.VMEM),
        scratch_shapes=[
            pltpu.VMEM((SLOTS, rows, depth), jnp.bfloat16),
            pltpu.VMEM((depth, TURNED), jnp.bfloat16),
            pltpu.VMEM((depth, rows), jnp.bfloat16),
            pltpu.VMEM((2, HALF), jnp.int32),
            pltpu.SMEM(member_count.shape, jnp.int32),
            pltpu.VMEM((2 * SLOTS, 8, HALF), jnp.int32),
            pltpu.VMEM((SLOTS, rows, HALF), jnp.int32),
            pltpu.VMEM((SLOTS, rows, HALF), jnp.float32),
            pltpu.VMEM((2 * SLOTS, 8, HALF), jnp.float32),
            pltpu.VMEM((2 * SLOTS, 8, HALF), jnp.float32),
            pltpu.SemaphoreType.DMA((CHUNKS,)),
            pltpu.SemaphoreType.DMA((2,)),
            pltpu.SemaphoreType.DMA((25,)),
            *[pltpu.SemaphoreType.DMA] * 6,
        ],
        compiler_params=pltpu.CompilerParams(collective_id=0, has_side_effects=True, vmem_limit_bytes=60 * 2**20),
        name="nearest_earlier",
    )(embeddings, member_order.reshape(2, HALF), member_count)
    return best.reshape(rows)


def solution(mesh):
    in_specs = (P(("grp", "row"), None), P(("grp", "row")), P())
    out_specs = P(("grp", "row"))
    return jax.shard_map(shards, mesh=mesh, in_specs=in_specs, out_specs=out_specs, check_vma=False)
```
